256 devices in a mesh: pipe: 8 (over x, y_hi), expert: 32 (over z, y_lo, core).
Axes of the slice: x: 4, y: 4 (y_hi: 2, y_lo: 2; y = y_hi * 2 + y_lo), z: 8, core: 2. Of those that a mesh axis runs over, the one named last changes fastest.
Arguments:
- forward_rows: bfloat16 [8, 2048, 7168], P('pipe', 'expert'), may hold values from -6 to 6
- forward_ids: int32 [8, 2048, 2], P('pipe', 'expert'), may hold values from 0 to 3, all different within a row; in each aligned block of 64 rows (0 to 63, 64 to 127, ..., all dimensions but the last counted through in order) at most 36 rows name the same one
- backward_rows: bfloat16 [8, 2048, 7168], P('pipe', 'expert'), may hold values from -6 to 6
- backward_ids: int32 [8, 2048, 2], P('pipe', 'expert'), may hold values from 0 to 3, all different within a row; in each aligned block of 64 rows (0 to 63, 64 to 127, ..., all dimensions but the last counted through in order) at most 36 rows name the same one
- backward_grad: bfloat16 [8, 2048, 7168], P('pipe', 'expert'), may hold values from -6 to 6
- backward_stash: bfloat16 [8, 2048, 2, 2, 1024], P('pipe', 'expert'), may hold values from -6 to 6
- router: bfloat16 [8, 4, 7168], P('pipe'), may hold values from -0.0625 to 0.0625
- w_gate: bfloat16 [8, 32, 7168, 128], P('pipe', 'expert'), may hold values from -0.0625 to 0.0625
- w_up: bfloat16 [8, 32, 7168, 128], P('pipe', 'expert'), may hold values from -0.0625 to 0.0625
- w_down: bfloat16 [8, 32, 128, 7168], P('pipe', 'expert'), may hold values from -0.1875 to 0.1875
Outputs:
- forward_next: bfloat16 [8, 2048, 7168], P('pipe', 'expert')
- backward_next: bfloat16 [8, 2048, 7168], P('pipe', 'expert')
- router_grad: float32 [8, 4, 7168], P('pipe')
The draws below stay inside these ranges and needn't reach their ends.
Inputs may be any that keep to these rules, and one draw needn't show every extreme that they name: `forward_ids`: among the rows of one device of the expert axis no expert is named by more than 36 rows, and in every draw some device names one expert exactly 36 times. The 2 experts of a row differ. `backward_ids`: among the rows of one device of the expert axis no expert is named by more than 36 rows, and in every draw some device names one expert exactly 36 times. The 2 experts of a row differ.
All inputs are finite; a program needn't handle non-finite values.
Results may differ from the reference program's by a relative error of at most 0.012.
Values may be sent and summed in bfloat16 or wider, within the bound.
No kernel may reach another device: no remote copies, remote signals or barrier semaphores. Data moves between devices by JAX's collectives and lax.ppermute only.
A program may use at most 192 MiB of HBM per device.

```python
import math
import jax
import jax.numpy as jnp
import numpy as np
from jax import lax

D = 7168
FF_EXP = 1024
EXPERTS = 4
TOP = 2
TOK_DEV = 64
GROUP = 8
HID_DEV = 128
SLICES = 32
TOKENS = 2048
CAP = 36
N_PIPE = 8
N_EXPERT = 32


def block_levels(stream_key, shape, cuts, low, largest):
    gain = 1.0
    for position, blocks in cuts:
        heights = jax.random.uniform(jax.random.fold_in(jax.random.fold_in(stream_key, 6), position), (blocks,), jnp.float32, low / len(cuts), largest / len(cuts))
        gain = gain * jnp.repeat(jnp.exp(heights), shape[position] // blocks).reshape((-1,) + (1,) * (len(shape) - 1 - position))
    return gain


def routed_block(own_key, own, number, rows, count, top, most, skew):
    sequence = jax.random.permutation(own_key, count)
    crowded, common = portions_of(count, rows * top, most, skew, True), portions_of(count, rows * top, most, skew, False)
    places = jnp.arange(count)

    def named(tallies, offset_by):
        used = int((tallies > 0).sum())
        fixed = max(1, used // 4)
        moved = fixed + (places - fixed + offset_by * (used - fixed)) % max(1, count - fixed)
        return jnp.zeros((count,), jnp.int32).at[sequence[jnp.where(places < fixed, places, moved)]].set(jnp.asarray(tallies, jnp.int32))

    tallies = jnp.where(number % 4 == 0, named(crowded, number // 4), named(common, number - number // 4 - 1))
    mixed = jax.random.permutation(jax.random.fold_in(own, 3), count)
    giver, receiver = mixed[0:count // 2 * 2:2], mixed[1:count // 2 * 2:2]
    slack = jnp.minimum(tallies[giver] - 1, most - tallies[receiver]) // 2
    slack = jnp.where((giver == sequence[0]) | (receiver == sequence[0]) | (tallies[receiver] == 0), 0, jnp.maximum(slack, 0))
    moved = jax.random.randint(jax.random.fold_in(own, 4), (count // 2,), 0, 1 << 20) % (slack + 1)
    tallies = tallies.at[giver].add(-moved).at[receiver].add(moved)
    labels = jnp.searchsorted(jnp.cumsum(tallies), jnp.arange(rows * top), side="right").astype(jnp.int32)
    grid = labels.reshape(top, rows).T
    grid = grid[jax.random.permutation(jax.random.fold_in(own, 1), rows)]
    offset_by = jax.random.randint(jax.random.fold_in(own, 2), (rows, 1), 0, top)
    return jnp.take_along_axis(grid, (jnp.arange(top)[None, :] + offset_by) % top, axis=1)


def portions_of(amount, total, reach, slope, full):
    weights = [(1 << 20) // math.isqrt(rank ** slope) + 1 for rank in range(1, amount + 1)]
    largest = reach if full else min(reach, max(-(-total // amount), total * weights[0] // sum(weights)))
    least = 1 if total - largest >= amount - 1 else 0
    holding, surplus = [largest] + [least] * (amount - 1), total - largest - least * (amount - 1)
    while surplus > 0:
        free = [i for i in range(1, amount) if holding[i] < largest] or [i for i in range(1, amount) if holding[i] < reach]
        pool, budget = sum([weights[i] for i in free]), surplus
        for i in free:
            extra = min(reach - holding[i], max(1, budget * weights[i] // pool), surplus)
            holding[i] = holding[i] + extra
            surplus = surplus - extra
    return np.array(holding)


def normal_values(rng, dims, spread, most, shards=(), held_as=jnp.bfloat16):
    factor_of = block_levels(rng, dims, shards, -0.22, 0.18) if shards else 1.0
    array = jax.random.normal(rng, dims, jnp.float32) * spread * factor_of
    return jnp.minimum(jnp.maximum(array, -most), most).astype(held_as)


def setup_inputs(seed: int = 0) -> dict:
    keys = jax.random.split(jax.random.key(seed), 11)
    forward_rows = normal_values(keys[0], (N_PIPE, TOKENS, D), 1.0, 6.0, ((0, 8), (1, 32)))
    forward_ids_keys = jax.random.split(jax.random.fold_in(keys[1], 1), N_PIPE * TOKENS // TOK_DEV)
    forward_ids_turns = jax.random.permutation(jax.random.fold_in(keys[1], 3), N_PIPE * TOKENS // TOK_DEV)
    forward_ids = jax.vmap(lambda own, number: routed_block(jax.random.fold_in(keys[1], 2), own, number, TOK_DEV, EXPERTS, TOP, CAP, 2))(forward_ids_keys, forward_ids_turns).reshape((N_PIPE, TOKENS, TOP))
    backward_rows = normal_values(keys[2], (N_PIPE, TOKENS, D), 1.0, 6.0, ((0, 8), (1, 32)))
    backward_ids_keys = jax.random.split(jax.random.fold_in(keys[3], 1), N_PIPE * TOKENS // TOK_DEV)
    backward_ids_turns = jax.random.permutation(jax.random.fold_in(keys[3], 3), N_PIPE * TOKENS // TOK_DEV)
    backward_ids = jax.vmap(lambda own, number: routed_block(jax.random.fold_in(keys[3], 2), own, number, TOK_DEV, EXPERTS, TOP, CAP, 2))(backward_ids_keys, backward_ids_turns).reshape((N_PIPE, TOKENS, TOP))
    backward_grad = normal_values(keys[4], (N_PIPE, TOKENS, D), 1.0, 6.0, ((0, 8), (1, 32)))
    backward_stash = normal_values(keys[5], (N_PIPE, TOKENS, TOP, 2, FF_EXP), 1.0, 6.0, ((0, 8), (1, 32)))
    router = normal_values(keys[6], (N_PIPE, EXPERTS, D), D ** -0.5, 0.0625, ((0, 8),))
    w_gate = normal_values(keys[7], (N_PIPE, SLICES, D, HID_DEV), D ** -0.5, 0.0625, ((0, 8), (1, 32)))
    w_up = normal_values(keys[8], (N_PIPE, SLICES, D, HID_DEV), D ** -0.5, 0.0625, ((0, 8), (1, 32)))
    w_down = normal_values(keys[9], (N_PIPE, SLICES, HID_DEV, D), FF_EXP ** -0.5, 0.1875, ((0, 8), (1, 32)))
    return {"forward_rows": forward_rows, "forward_ids": forward_ids, "backward_rows": backward_rows, "backward_ids": backward_ids, "backward_grad": backward_grad, "backward_stash": backward_stash, "router": router, "w_gate": w_gate, "w_up": w_up, "w_down": w_down}


ROUTE_SCALE = 2.5


def silu_slope(pre_act):
    sigmoid_v = jax.nn.sigmoid(pre_act)
    return sigmoid_v * (1.0 + pre_act * (1.0 - sigmoid_v))


def rounded(pre_act):
    return lax.optimization_barrier(pre_act.astype(jnp.bfloat16)).astype(jnp.float32)


def gate_terms(tok_rows, ids, router):
    logits = lax.dot_general(tok_rows, router, (((1,), (1,)), ((), ())), preferred_element_type=jnp.float32)
    one_hot = (ids[:, :, None] == jnp.arange(EXPERTS, dtype=jnp.int32)[None, None, :]).astype(jnp.float32)
    probs_m = jax.nn.sigmoid(jnp.sum(one_hot * logits[:, None, :], axis=2))
    total_m = jnp.sum(probs_m, axis=1, keepdims=True)
    return one_hot, probs_m, total_m


def slot_index(ids):
    one_hot = (ids[:, :, None] == jnp.arange(EXPERTS, dtype=jnp.int32)[None, None, :]).astype(jnp.int32)
    one_hot = one_hot.reshape(N_EXPERT, TOK_DEV * TOP, EXPERTS)
    before = jnp.cumsum(one_hot, axis=1) - one_hot
    rank_of = jnp.sum(before * one_hot, axis=2).reshape(TOKENS * TOP)
    source_of = jnp.arange(TOKENS * TOP, dtype=jnp.int32) // (TOK_DEV * TOP)
    return (ids.reshape(TOKENS * TOP) * (N_EXPERT * CAP) + source_of * CAP + rank_of).astype(jnp.int32)


def expert_forward(tok_rows, gate_w, up_w, down_w):
    rows_wide = tok_rows.astype(jnp.float32)
    pre_gate = jnp.einsum("rd,gdh->rgh", rows_wide, gate_w.astype(jnp.float32))
    pre_up = jnp.einsum("rd,gdh->rgh", rows_wide, up_w.astype(jnp.float32))
    hidden = rounded(jax.nn.silu(pre_gate) * pre_up)
    member_parts = jnp.einsum("rgh,ghd->grd", hidden, down_w.astype(jnp.float32))
    return jnp.sum(rounded(member_parts), axis=0)


def expert_backward(grad_rows, scales, stash_rows, gate_w, up_w, down_w):
    grads_wide = grad_rows.astype(jnp.float32)
    pre_gate = stash_rows[:, 0].astype(jnp.float32)
    pre_up = stash_rows[:, 1].astype(jnp.float32)
    activated = jax.nn.silu(pre_gate)
    hidden = rounded(activated * pre_up)
    down_wide = down_w.astype(jnp.float32)
    member_parts = jnp.einsum("rgh,ghd->grd", hidden, down_wide)
    inner_b = jnp.sum(rounded(jnp.sum(member_parts * grads_wide[None], axis=2)), axis=0)
    back_grad = jnp.einsum("rd,ghd->rgh", grads_wide, down_wide) * scales.astype(jnp.float32)[:, None, None]
    d_gate = rounded(back_grad * pre_up * silu_slope(pre_gate))
    d_up = rounded(back_grad * activated)
    d_parts = jnp.einsum("rgh,gdh->grd", d_gate, gate_w.astype(jnp.float32))
    d_parts = d_parts + jnp.einsum("rgh,gdh->grd", d_up, up_w.astype(jnp.float32))
    return jnp.sum(rounded(d_parts), axis=0), inner_b


def one_section(pieces):
    fwd_rows, fwd_ids, bwd_rows, bwd_ids, bwd_grad, bwd_stash, router, gate_all, up_all, down_all = pieces
    gate_w = gate_all.reshape(EXPERTS, GROUP, D, HID_DEV)
    up_w = up_all.reshape(EXPERTS, GROUP, D, HID_DEV)
    down_w = down_all.reshape(EXPERTS, GROUP, HID_DEV, D)
    slot_total = EXPERTS * N_EXPERT * CAP
    per_expert = N_EXPERT * CAP

    one_hot_f, probs_f, total_f = gate_terms(fwd_rows, fwd_ids, router)
    weights_f = ROUTE_SCALE * probs_f / total_f
    slot_f = slot_index(fwd_ids)
    buffer_f = jnp.zeros((slot_total, D), jnp.bfloat16).at[slot_f].set(jnp.repeat(fwd_rows, TOP, axis=0))
    buffer_f = buffer_f.reshape(EXPERTS, per_expert, D)
    results_f = jnp.concatenate([expert_forward(buffer_f[expert_idx], gate_w[expert_idx], up_w[expert_idx], down_w[expert_idx]) for expert_idx in range(EXPERTS)], axis=0)
    picked_f = results_f[slot_f].reshape(TOKENS, TOP, D)
    layer_out = (fwd_rows.astype(jnp.float32) + jnp.sum(weights_f[:, :, None] * picked_f, axis=1)).astype(jnp.bfloat16)

    one_hot_b, probs_b, total_b = gate_terms(bwd_rows, bwd_ids, router)
    share_b = probs_b / total_b
    scale_b = (ROUTE_SCALE * share_b).astype(jnp.bfloat16)
    slot_b = slot_index(bwd_ids)
    grad_buf = jnp.zeros((slot_total, D), jnp.bfloat16).at[slot_b].set(jnp.repeat(bwd_grad, TOP, axis=0))
    grad_buf = grad_buf.reshape(EXPERTS, per_expert, D)
    scale_buf = jnp.zeros((slot_total,), jnp.bfloat16).at[slot_b].set(scale_b.reshape(TOKENS * TOP))
    scale_buf = scale_buf.reshape(EXPERTS, per_expert)
    stash_flat = bwd_stash.reshape(TOKENS * TOP, 2, GROUP, HID_DEV)
    stash_buf = jnp.zeros((slot_total, 2, GROUP, HID_DEV), jnp.bfloat16).at[slot_b].set(stash_flat)
    stash_buf = stash_buf.reshape(EXPERTS, per_expert, 2, GROUP, HID_DEV)
    d_sums = []
    inner_sums = []
    for expert_idx in range(EXPERTS):
        d_rows, inner_rows = expert_backward(grad_buf[expert_idx], scale_buf[expert_idx], stash_buf[expert_idx], gate_w[expert_idx], up_w[expert_idx], down_w[expert_idx])
        d_sums.append(d_rows)
        inner_sums.append(inner_rows)
    d_all = jnp.concatenate(d_sums, axis=0)
    inner_all = jnp.concatenate(inner_sums, axis=0)
    d_expert = jnp.sum(d_all[slot_b].reshape(TOKENS, TOP, D), axis=1)
    inner_b = inner_all[slot_b].reshape(TOKENS, TOP)
    d_logit = ROUTE_SCALE / total_b * (inner_b - jnp.sum(share_b * inner_b, axis=1, keepdims=True)) * probs_b * (1.0 - probs_b)
    score_grad = jnp.sum(one_hot_b * d_logit[:, :, None], axis=1)
    router_wide = router.astype(jnp.float32)
    router_part = jnp.dot(score_grad, router_wide, precision=lax.Precision.HIGHEST)
    input_grad = (bwd_grad.astype(jnp.float32) + d_expert + router_part).astype(jnp.bfloat16)
    router_grad = jnp.dot(score_grad.T, bwd_rows.astype(jnp.float32), precision=lax.Precision.HIGHEST) / TOKENS
    return layer_out, input_grad, router_grad


def reference(forward_rows, forward_ids, backward_rows, backward_ids, backward_grad, backward_stash, router, w_gate, w_up, w_down):
    layer_out, input_grad, router_grad = lax.map(one_section, (forward_rows, forward_ids, backward_rows, backward_ids, backward_grad, backward_stash, router, w_gate, w_up, w_down))
    return jnp.roll(layer_out, 1, axis=0), jnp.roll(input_grad, -1, axis=0), router_grad
```

```python
import jax
import jax.numpy as jnp
from jax import lax
from jax.experimental import pallas as pl
from jax.experimental.pallas import tpu as pltpu
from jax.sharding import PartitionSpec as P

CAP = 40
USED = 36
ROUTE_SCALE = 2.5
BF = jnp.bfloat16
F32 = jnp.float32
VMEM_BYTES = 48 * 1024 * 1024


def params(steps):
    return pltpu.CompilerParams(
        dimension_semantics=("arbitrary",) * steps, vmem_limit_bytes=VMEM_BYTES
    )


def shifted(block, axis, distance):
    devices = range(lax.axis_size(axis))
    route = [((i - distance) % len(devices), i) for i in devices]
    return lax.ppermute(block, axis, route)


def exchanged(block, mask):
    route = [(i, i ^ mask) for i in range(lax.axis_size("expert"))]
    return lax.ppermute(block, "expert", route)


def all_to_all(block):
    return lax.all_to_all(block, "expert", split_axis=0, concat_axis=0, tiled=True)


def gate_terms(tok_rows, ids, router_rows):
    experts = router_rows.shape[0]
    logits = lax.dot_general(
        tok_rows, router_rows, (((1,), (1,)), ((), ())), preferred_element_type=F32
    )
    one_hot = (ids[:, :, None] == jnp.arange(experts, dtype=jnp.int32)[None, None, :]).astype(F32)
    probs_m = jax.nn.sigmoid(jnp.sum(one_hot * logits[:, None, :], axis=2))
    total_m = jnp.sum(probs_m, axis=1, keepdims=True)
    return one_hot, probs_m, total_m


def route_plan(ids, experts):
    tokens, top = ids.shape
    flat_ids = ids.reshape(tokens * top)
    one_hot = (flat_ids[:, None] == jnp.arange(experts, dtype=jnp.int32)[None, :]).astype(jnp.int32)
    before = jnp.cumsum(one_hot, axis=0) - one_hot
    slot = flat_ids * CAP + jnp.sum(before * one_hot, axis=1)
    return slot.reshape(tokens, top)


def pack_forward(select, rows, experts, group):
    tokens, features = rows.shape
    width = features // group
    slots = select.shape[0]

    def body(select_ref, rows_ref, out_ref):
        got = jnp.dot(select_ref[...], rows_ref[...], preferred_element_type=F32)
        out_ref[:, 0] = got.reshape(experts, CAP, width).astype(BF)

    return pl.pallas_call(
        body,
        grid=(group,),
        in_specs=[
            pl.BlockSpec((slots, tokens), lambda g: (0, 0)),
            pl.BlockSpec((tokens, width), lambda g: (0, g)),
        ],
        out_specs=pl.BlockSpec((experts, 1, CAP, width), lambda g: (0, g, 0, 0)),
        out_shape=jax.ShapeDtypeStruct((experts, group, CAP, width), BF),
        compiler_params=params(1),
        name="pack_forward",
    )(select, rows)


def pack_backward(select, select_pairs, rows, stash, experts, group, hidden):
    tokens, features = rows.shape
    width = features // group
    slots, pairs = select_pairs.shape

    def body(select_ref, pairs_ref, rows_ref, gate_ref, up_ref, out_ref):
        got = jnp.dot(select_ref[...], rows_ref[...], preferred_element_type=F32)
        out_ref[:, 0, :, 0:width] = got.reshape(experts, CAP, width).astype(BF)
        for place, ref in enumerate((gate_ref, up_ref)):
            got = jnp.dot(pairs_ref[...], ref[...], preferred_element_type=F32)
            start = width + place * hidden
            out_ref[:, 0, :, start : start + hidden] = got.reshape(experts, CAP, hidden).astype(BF)

    return pl.pallas_call(
        body,
        grid=(group,),
        in_specs=[
            pl.BlockSpec((slots, tokens), lambda g: (0, 0)),
            pl.BlockSpec((slots, pairs), lambda g: (0, 0)),
            pl.BlockSpec((tokens, width), lambda g: (0, g)),
            pl.BlockSpec((pairs, hidden), lambda g: (0, g)),
            pl.BlockSpec((pairs, hidden), lambda g: (0, group + g)),
        ],
        out_specs=pl.BlockSpec((experts, 1, CAP, width + 2 * hidden), lambda g: (0, g, 0, 0)),
        out_shape=jax.ShapeDtypeStruct((experts, group, CAP, width + 2 * hidden), BF),
        compiler_params=params(1),
        name="pack_backward",
    )(select, select_pairs, rows, stash, stash)


def contract(left, right, right_dim):
    return lax.dot_general(left, right, (((1,), (right_dim,)), ((), ())), preferred_element_type=F32)


def first_stage(own, other, weights, width, hidden, right_dim, name):
    rows = own.shape[0]
    block = 256

    def body(own_ref, other_ref, *refs):
        for w_ref, out_ref in zip(refs[:4], refs[4:]):
            total = contract(own_ref[...], w_ref[0], right_dim)
            total += contract(other_ref[...], w_ref[1], right_dim)
            out_ref[...] = total.astype(out_ref.dtype)

    return pl.pallas_call(
        body,
        grid=(rows // block,),
        in_specs=[pl.BlockSpec((block, width), lambda r: (r, 0))] * 2
        + [pl.BlockSpec(weights[0].shape, lambda r: (0, 0, 0))] * 4,
        out_specs=[pl.BlockSpec((block, hidden), lambda r: (r, 0))] * 4,
        out_shape=[jax.ShapeDtypeStruct((rows, hidden), F32)]
        + [jax.ShapeDtypeStruct((rows, hidden), BF)] * 3,
        compiler_params=params(1),
        name=name,
    )(own, other, *weights)


def second_stage(pieces, weights, width, right_dim, name):
    rows, hidden = pieces[0].shape
    block = 256

    def body(*refs):
        for half, out_ref in enumerate(refs[8:]):
            total = contract(refs[0][...], refs[4][half], right_dim)
            for step in range(1, 4):
                total += contract(refs[step][...], refs[4 + step][half], right_dim)
            out_ref[...] = total.astype(BF)

    return pl.pallas_call(
        body,
        grid=(rows // block,),
        in_specs=[pl.BlockSpec((block, hidden), lambda r: (r, 0))] * 4
        + [pl.BlockSpec(weights[0].shape, lambda r: (0, 0, 0))] * 4,
        out_specs=[pl.BlockSpec((block, width), lambda r: (r, 0))] * 2,
        out_shape=[jax.ShapeDtypeStruct((rows, width), BF)] * 2,
        compiler_params=params(1),
        name=name,
    )(*pieces, *weights)


def combine(picks, factors, returned, rows, extra, name):
    tokens, features = rows.shape
    experts, group, cap, width = returned.shape
    top = len(picks)

    def body(*refs):
        pick_refs, factor_ref, back_ref, rows_ref = refs[:top], refs[top], refs[top + 1], refs[top + 2]
        out_ref = refs[-1]
        back = back_ref[:, 0].astype(F32).reshape(experts * cap, width).astype(BF)
        total = rows_ref[...].astype(F32)
        for k in range(top):
            picked = jnp.dot(pick_refs[k][...], back, preferred_element_type=F32)
            total += factor_ref[:, k : k + 1] * picked
        if extra is not None:
            score_ref, router_ref = refs[top + 3 : top + 5]
            for e in range(experts):
                total += score_ref[:, e : e + 1] * router_ref[e : e + 1, :].astype(F32)
        out_ref[...] = total.astype(BF)

    in_specs = [pl.BlockSpec(picks[0].shape, lambda g: (0, 0))] * top + [
        pl.BlockSpec(factors.shape, lambda g: (0, 0)),
        pl.BlockSpec((experts, 1, cap, width), lambda g: (0, g, 0, 0)),
        pl.BlockSpec((tokens, width), lambda g: (0, g)),
    ]
    operands = list(picks) + [factors, returned, rows]
    if extra is not None:
        in_specs += [
            pl.BlockSpec(extra[0].shape, lambda g: (0, 0)),
            pl.BlockSpec((experts, width), lambda g: (0, g)),
        ]
        operands += list(extra)
    return pl.pallas_call(
        body,
        grid=(group,),
        in_specs=in_specs,
        out_specs=pl.BlockSpec((tokens, width), lambda g: (0, g)),
        out_shape=jax.ShapeDtypeStruct((tokens, features), BF),
        compiler_params=params(1),
        name=name,
    )(*operands)


def silu_slope(pre_act):
    sigmoid_v = jax.nn.sigmoid(pre_act)
    return sigmoid_v * (1.0 + pre_act * (1.0 - sigmoid_v))


def shards(
    forward_rows,
    forward_ids,
    backward_rows,
    backward_ids,
    backward_grad,
    backward_stash,
    router,
    w_gate,
    w_up,
    w_down,
):
    fwd_rows, fwd_ids = forward_rows[0], forward_ids[0]
    bwd_rows, bwd_ids, bwd_grad = backward_rows[0], backward_ids[0], backward_grad[0]
    router_rows = router[0]
    gate_w, up_w, down_w = w_gate[0, 0], w_up[0, 0], w_down[0, 0]
    members = lax.axis_size("expert")
    experts, features = router_rows.shape
    group = members // experts
    hidden = down_w.shape[0]
    width = features // group
    tokens, top = fwd_ids.shape
    slots = experts * CAP
    place = lax.axis_index("expert") % group
    core = place % 2
    chip = place // 2
    slot_axis = jnp.arange(slots, dtype=jnp.int32)

    down_split = jnp.transpose(down_w.reshape(hidden, group, width), (1, 0, 2))
    joined_split = jnp.concatenate([gate_w, up_w], axis=1).reshape(group, width, 2 * hidden)

    def halves(split, step):
        first = 2 * (chip ^ step) + core
        second = 2 * (chip ^ step) + 1 - core
        return jnp.concatenate(
            [
                lax.dynamic_slice_in_dim(split, first, 1, 0),
                lax.dynamic_slice_in_dim(split, second, 1, 0),
            ],
            axis=0,
        )

    downs = [exchanged(halves(down_split, s), 2 * s) if s else halves(down_split, s) for s in range(4)]
    joins = [
        exchanged(halves(joined_split, s), 2 * s) if s else halves(joined_split, s) for s in range(4)
    ]

    slot_b = route_plan(bwd_ids, experts)
    pairs_b = (slot_axis[:, None] == slot_b.reshape(1, tokens * top)).astype(BF)
    select_b = jnp.sum(slot_axis[:, None, None] == slot_b[None], axis=2).astype(BF)
    stash = backward_stash[0].reshape(tokens * top, 2 * group * hidden)
    send_b = pack_backward(select_b, pairs_b, bwd_grad, stash, experts, group, hidden)
    got_b = all_to_all(send_b.reshape(members, CAP, width + 2 * hidden))
    got_b = got_b.reshape(members * CAP, width + 2 * hidden)

    slot_f = route_plan(fwd_ids, experts)
    select_f = jnp.sum(slot_axis[:, None, None] == slot_f[None], axis=2).astype(BF)
    send_f = pack_forward(select_f, fwd_rows, experts, group)
    got_f = all_to_all(send_f.reshape(members, CAP, width)).reshape(members * CAP, width)

    own_b = got_b[:, :width]
    raw_parts = first_stage(own_b, exchanged(own_b, 1), downs, width, hidden, 1, "raw_grad")
    raw_grad = raw_parts[0]
    for s in range(1, 4):
        raw_grad = raw_grad + exchanged(raw_parts[s], 2 * s).astype(F32)
    pre_gate = got_b[:, width : width + hidden].astype(F32)
    pre_up = got_b[:, width + hidden :].astype(F32)
    activated = jax.nn.silu(pre_gate)
    hidden_b = (activated * pre_up).astype(BF).astype(F32)
    inner_part = jnp.sum(hidden_b * raw_grad, axis=1).astype(BF)
    d_gate = (raw_grad * pre_up * silu_slope(pre_gate)).astype(BF)
    d_up = (raw_grad * activated).astype(BF)
    d_own = jnp.concatenate([d_gate, d_up], axis=1)
    d_pieces = [d_own] + [exchanged(d_own, 2 * s) for s in range(1, 4)]
    d_keep, d_give = second_stage(d_pieces, joins, width, 1, "d_rows")
    d_sum = (d_keep.astype(F32) + exchanged(d_give, 1).astype(F32)).astype(BF)
    d_sum = d_sum.reshape(members, CAP, width)
    inner_row = jnp.pad(inner_part.reshape(members, 1, CAP), ((0, 0), (0, 0), (0, width - CAP)))
    is_inner = lax.broadcasted_iota(jnp.int32, (1, CAP, 1), 1) == USED
    d_sum = jnp.where(is_inner, inner_row, d_sum)
    back_b = all_to_all(d_sum).reshape(experts, group, CAP, width)

    pre_parts = first_stage(got_f, exchanged(got_f, 1), joins, width, 2 * hidden, 0, "pre_acts")
    pre_acts = pre_parts[0]
    for s in range(1, 4):
        pre_acts = pre_acts + exchanged(pre_parts[s], 2 * s).astype(F32)
    hidden_f = (jax.nn.silu(pre_acts[:, :hidden]) * pre_acts[:, hidden:]).astype(BF)
    hidden_pieces = [hidden_f] + [exchanged(hidden_f, 2 * s) for s in range(1, 4)]
    y_keep, y_give = second_stage(hidden_pieces, downs, width, 0, "y_rows")
    y_sum = (y_keep.astype(F32) + exchanged(y_give, 1).astype(F32)).astype(BF)
    back_f = all_to_all(y_sum.reshape(members, CAP, width)).reshape(experts, group, CAP, width)

    one_hot_b, probs_b, total_b = gate_terms(bwd_rows, bwd_ids, router_rows)
    share_b = probs_b / total_b
    scale_b = (ROUTE_SCALE * share_b).astype(BF).astype(F32)
    picks_b = [(slot_b[:, k : k + 1] == slot_axis[None, :]).astype(BF) for k in range(top)]
    inner_all = jnp.sum(back_b[:, :, USED, :CAP].astype(F32), axis=1).reshape(1, slots)
    inner_sum = jnp.stack(
        [jnp.sum(picks_b[k].astype(F32) * inner_all, axis=1) for k in range(top)], axis=1
    )
    d_logit = (
        ROUTE_SCALE
        / total_b
        * (inner_sum - jnp.sum(share_b * inner_sum, axis=1, keepdims=True))
        * probs_b
        * (1.0 - probs_b)
    )
    score_grad = jnp.sum(one_hot_b * d_logit[:, :, None], axis=1)
    input_grad = combine(
        picks_b, scale_b, back_b, bwd_grad, (score_grad, router_rows), "combine_backward"
    )
    router_total = jnp.dot(score_grad.T, bwd_rows.astype(F32), precision=lax.Precision.HIGHEST)
    router_total = router_total * (1.0 / (tokens * members))
    mask = 1
    while mask < members:
        router_total = router_total + exchanged(router_total, mask)
        mask *= 2
    backward_out_rows = shifted(input_grad, "pipe", -1)

    one_hot_f, probs_f, total_f = gate_terms(fwd_rows, fwd_ids, router_rows)
    weights_f = ROUTE_SCALE * probs_f / total_f
    picks_f = [(slot_f[:, k : k + 1] == slot_axis[None, :]).astype(BF) for k in range(top)]
    layer_out = combine(picks_f, weights_f, back_f, fwd_rows, None, "combine_forward")
    forward_out_rows = shifted(layer_out, "pipe", 1)
    return (forward_out_rows[None], backward_out_rows[None], router_total[None])


def solution(mesh):
    return jax.shard_map(
        shards,
        mesh=mesh,
        in_specs=(
            P("pipe", "expert", None),
            P("pipe", "expert", None),
            P("pipe", "expert", None),
            P("pipe", "expert", None),
            P("pipe", "expert", None),
            P("pipe", "expert", None, None, None),
            P("pipe", None, None),
            P("pipe", "expert", None, None),
            P("pipe", "expert", None, None),
            P("pipe", "expert", None, None),
        ),
        out_specs=(P("pipe", "expert", None), P("pipe", "expert", None), P("pipe", None, None)),
        check_vma=False,
    )
```

```python
import jax
import jax.numpy as jnp
from jax import lax
from jax.experimental import pallas as pl
from jax.experimental.pallas import tpu as pltpu
from jax.sharding import PartitionSpec as P

CAP = 40
ROUTE_SCALE = 2.5
BF = jnp.bfloat16
F32 = jnp.float32
USED = 36
VMEM_BYTES = 48 * 1024 * 1024


def params(steps):
    return pltpu.CompilerParams(
        dimension_semantics=("arbitrary",) * steps, vmem_limit_bytes=VMEM_BYTES
    )


def shifted(block, axis, distance):
    devices = range(lax.axis_size(axis))
    route = [((i - distance) % len(devices), i) for i in devices]
    return lax.ppermute(block, axis, route)


def exchanged(block, mask):
    route = [(i, i ^ mask) for i in range(lax.axis_size("expert"))]
    return lax.ppermute(block, "expert", route)


def all_to_all(block):
    return lax.all_to_all(block, "expert", split_axis=0, concat_axis=0, tiled=True)


def piece_route(piece):
    members = lax.axis_size("expert")
    step = (0, 2, -1, -3)[piece]
    return [(i, (i + 4 * (step if i // 4 % 2 == 0 else -step)) % members) for i in range(members)]


def hopped(block, piece):
    return lax.ppermute(block, "expert", piece_route(piece))


def to_source(block, piece):
    if not piece:
        return block
    return lax.ppermute(block, "expert", [(b, a) for a, b in piece_route(piece)])


def gate_terms(tok_rows, ids, router_rows):
    experts = router_rows.shape[0]
    logits = lax.dot_general(
        tok_rows, router_rows, (((1,), (1,)), ((), ())), preferred_element_type=F32
    )
    one_hot = (ids[:, :, None] == jnp.arange(experts, dtype=jnp.int32)[None, None, :]).astype(F32)
    probs_m = jax.nn.sigmoid(jnp.sum(one_hot * logits[:, None, :], axis=2))
    total_m = jnp.sum(probs_m, axis=1, keepdims=True)
    return one_hot, probs_m, total_m


def route_plan(ids, experts, level):
    tokens, top = ids.shape
    flat_ids = ids.reshape(tokens * top)
    one_hot = (flat_ids[:, None] == jnp.arange(experts, dtype=jnp.int32)[None, :]).astype(jnp.int32)
    before = jnp.cumsum(one_hot, axis=0) - one_hot
    rank = jnp.sum(before * one_hot, axis=1)
    ahead = flat_ids - level // 2
    ahead = jnp.where(level % 2 == 0, ahead, -ahead) % experts
    piece = jnp.where(ahead == 2, 3, jnp.where(ahead == 3, 2, ahead))
    return (piece * CAP + rank).reshape(tokens, top)


def pack(core, select_f, select_b, select_pairs, rows_f, rows_b, stash, hidden):
    tokens, features = rows_f.shape
    slots, pairs = select_pairs.shape
    lanes = stash.shape[1]
    quarter = lanes // 4
    chips = quarter // hidden
    total = 2 * features + lanes
    block = total // 4

    def body(core_ref, f_ref, b_ref, pairs_ref, rows_f_ref, rows_b_ref, stash_ref, *out_refs):
        def spread(select_ref, source, at):
            got = jnp.dot(select_ref[...], source, preferred_element_type=F32)
            for k in range(2):
                half = got[k * slots // 2 : (k + 1) * slots // 2]
                out_refs[k][:, at : at + source.shape[1]] = half.astype(BF)

        def fill(step):
            first, last = step * block, (step + 1) * block
            for select_ref, ref, start in ((f_ref, rows_f_ref, 0), (b_ref, rows_b_ref, features)):
                low, high = max(first, start), min(last, start + features)
                if low < high:
                    spread(select_ref, ref[:, low - start : high - start], low - first)
            for place in range(4 * chips):
                at = 2 * features + place * hidden
                if first <= at < last:
                    owner = (core_ref[0] + 1 + place // (2 * chips)) % 2
                    part, chip = place // chips % 2, place % chips
                    start = part * 2 * quarter + (2 * chip + owner) * hidden
                    source = stash_ref[:, pl.ds(pl.multiple_of(start, hidden), hidden)]
                    spread(pairs_ref, source, at - first)

        for step in range(4):
            pl.when(pl.program_id(0) == step)(lambda step=step: fill(step))

    def whole(array):
        return pl.BlockSpec(array.shape, lambda j: (0, 0))

    return pl.pallas_call(
        body,
        grid=(4,),
        in_specs=[pl.BlockSpec(memory_space=pltpu.SMEM)]
        + [whole(a) for a in (select_f, select_b, select_pairs, rows_f, rows_b, stash)],
        out_specs=[pl.BlockSpec((slots // 2, block), lambda j: (0, j))] * 2,
        out_shape=[jax.ShapeDtypeStruct((slots // 2, total), BF)] * 2,
        compiler_params=params(1),
        name="pack",
    )(core, select_f, select_b, select_pairs, rows_f, rows_b, stash)


def contract(left, right, right_dim):
    return lax.dot_general(left, right, (((1,), (right_dim,)), ((), ())), preferred_element_type=F32)


def silu_slope(pre_act):
    sigmoid_v = jax.nn.sigmoid(pre_act)
    return sigmoid_v * (1.0 + pre_act * (1.0 - sigmoid_v))


def backward_first(chip, parts, downs):
    rows = parts[0].shape[0]
    chips, count = len(downs), len(parts)
    hidden, features = downs[0].shape
    block = 1792
    steps = features // block
    wide = 2 * chips * hidden

    def body(chip_ref, *refs):
        row_refs, stash_refs, refs = refs[:count], refs[count : 2 * count], refs[2 * count :]
        w_refs, (d_ref, inner_ref, total) = refs[:chips], refs[chips:]
        step = pl.program_id(0)
        left = jnp.concatenate([ref[...] for ref in row_refs], axis=0)
        right = jnp.concatenate([ref[...] for ref in w_refs], axis=0)
        got = contract(left, right, 1)

        @pl.when(step == 0)
        def _():
            total[...] = got

        @pl.when(step > 0)
        def _():
            total[...] += got

        @pl.when(step == steps - 1)
        def _():
            for part, stash_ref in enumerate(stash_refs):
                place = slice(part * rows, (part + 1) * rows)
                inner = jnp.zeros((rows, 1), F32)
                for s in range(chips):
                    start = (chip_ref[0] ^ s) * hidden
                    pre_gate = stash_ref[:, pl.ds(pl.multiple_of(start, hidden), hidden)].astype(F32)
                    start = start + chips * hidden
                    pre_up = stash_ref[:, pl.ds(pl.multiple_of(start, hidden), hidden)].astype(F32)
                    raw = total[place, s * hidden : (s + 1) * hidden]
                    sigmoid_v = jax.nn.sigmoid(pre_gate)
                    activated = pre_gate * sigmoid_v
                    slope = sigmoid_v * (1.0 + pre_gate * (1.0 - sigmoid_v))
                    hidden_b = (activated * pre_up).astype(BF).astype(F32)
                    inner += jnp.sum(hidden_b * raw, axis=1, keepdims=True)
                    at = 2 * s * hidden
                    d_ref[place, at : at + hidden] = (raw * pre_up * slope).astype(BF)
                    d_ref[place, at + hidden : at + 2 * hidden] = (raw * activated).astype(BF)
                inner_ref[place, :] = jnp.broadcast_to(inner, (rows, 128))

    return pl.pallas_call(
        body,
        grid=(steps,),
        in_specs=[pl.BlockSpec(memory_space=pltpu.SMEM)]
        + [pl.BlockSpec((rows, block), lambda j: (0, steps + j))] * count
        + [pl.BlockSpec((rows, wide), lambda j: (0, 2 * features // wide + 1))] * (count // 2)
        + [pl.BlockSpec((rows, wide), lambda j: (0, 2 * features // wide))] * (count // 2)
        + [pl.BlockSpec((hidden, block), lambda j: (0, j))] * chips,
        out_specs=[
            pl.BlockSpec((count * rows, 2 * chips * hidden), lambda j: (0, 0)),
            pl.BlockSpec((count * rows, 128), lambda j: (0, 0)),
        ],
        out_shape=[
            jax.ShapeDtypeStruct((count * rows, 2 * chips * hidden), BF),
            jax.ShapeDtypeStruct((count * rows, 128), F32),
        ],
        scratch_shapes=[pltpu.VMEM((count * rows, chips * hidden), F32)],
        compiler_params=params(1),
        name="backward_first",
    )(chip, *parts, *parts, *downs)


def backward_second(d_joined, weights):
    rows = d_joined.shape[0] // 2
    features, joined = weights[0].shape
    chips = len(weights)
    block = 1792

    def body(d_ref, *refs):
        keep_ref, give_ref = refs[chips:]
        right = jnp.concatenate([ref[...] for ref in refs[:chips]], axis=1)
        got = contract(d_ref[...], right, 1)
        keep_ref[...] = got[:rows].astype(BF)
        give_ref[...] = got[rows:].astype(BF)

    return pl.pallas_call(
        body,
        grid=(features // block,),
        in_specs=[pl.BlockSpec(d_joined.shape, lambda j: (0, 0))]
        + [pl.BlockSpec((block, joined), lambda j: (j, 0))] * chips,
        out_specs=[pl.BlockSpec((rows, block), lambda j: (0, j))] * 2,
        out_shape=[jax.ShapeDtypeStruct((rows, features), BF)] * 2,
        compiler_params=params(1),
        name="backward_second",
    )(d_joined, *weights)


def forward_first(parts, weights):
    rows, count = parts[0].shape[0], len(parts)
    features, joined = weights[0].shape
    chips = len(weights)
    hidden = joined // 2
    block = 1792
    steps = features // block

    def body(*refs):
        row_refs, refs = refs[:count], refs[count:]
        out_ref, total = refs[chips:]
        step = pl.program_id(0)
        right = jnp.concatenate([ref[...] for ref in refs[:chips]], axis=1)
        left = jnp.concatenate([ref[...] for ref in row_refs], axis=0)
        got = contract(left, right, 0)

        @pl.when(step == 0)
        def _():
            total[...] = got

        @pl.when(step > 0)
        def _():
            total[...] += got

        @pl.when(step == steps - 1)
        def _():
            for s in range(chips):
                at = 2 * s * hidden
                gate = total[:, at : at + hidden]
                up = total[:, at + hidden : at + 2 * hidden]
                out_ref[:, s * hidden : (s + 1) * hidden] = (jax.nn.silu(gate) * up).astype(BF)

    return pl.pallas_call(
        body,
        grid=(steps,),
        in_specs=[pl.BlockSpec((rows, block), lambda j: (0, j))] * count
        + [pl.BlockSpec((block, joined), lambda j: (j, 0))] * chips,
        out_specs=pl.BlockSpec((count * rows, chips * hidden), lambda j: (0, 0)),
        out_shape=jax.ShapeDtypeStruct((count * rows, chips * hidden), BF),
        scratch_shapes=[pltpu.VMEM((count * rows, chips * joined), F32)],
        compiler_params=params(1),
        name="forward_first",
    )(*parts, *weights)


def forward_second(hidden_f, downs):
    rows = hidden_f.shape[0] // 2
    hidden, features = downs[0].shape
    chips = len(downs)
    block = 1792

    def body(hidden_ref, *refs):
        keep_ref, give_ref = refs[chips:]
        right = jnp.concatenate([ref[...] for ref in refs[:chips]], axis=0)
        got = contract(hidden_ref[...], right, 0)
        keep_ref[...] = got[:rows].astype(BF)
        give_ref[...] = got[rows:].astype(BF)

    return pl.pallas_call(
        body,
        grid=(features // block,),
        in_specs=[pl.BlockSpec(hidden_f.shape, lambda j: (0, 0))]
        + [pl.BlockSpec((hidden, block), lambda j: (0, j))] * chips,
        out_specs=[pl.BlockSpec((rows, block), lambda j: (0, j))] * 2,
        out_shape=[jax.ShapeDtypeStruct((rows, features), BF)] * 2,
        compiler_params=params(1),
        name="forward_second",
    )(hidden_f, *downs)


def merged(keep, swapped):
    total = (keep.astype(F32) + swapped.astype(F32)).astype(BF)
    return [total[place * CAP : (place + 1) * CAP] for place in (0, 2, 1, 3)]


def combine(picks, factors, returned, rows, extra, name):
    tokens = rows.shape[0]
    features = returned[0].shape[1]
    block = 3584
    top, pieces = len(picks), len(returned)
    slots = picks[0].shape[1]

    def body(*refs):
        pick_refs, factor_ref, refs = refs[:top], refs[top], refs[top + 1 :]
        back_refs, rows_ref, refs = refs[:pieces], refs[pieces], refs[pieces + 1 :]
        out_ref = refs[-1]
        back = jnp.concatenate([ref[...].astype(F32) for ref in back_refs], axis=0).astype(BF)
        total = rows_ref[...].astype(F32)
        for k in range(top):
            picked = jnp.dot(pick_refs[k][...], back, preferred_element_type=F32)
            total += factor_ref[:, k : k + 1] * picked
        if extra is not None:
            score_ref, router_ref = refs[:2]
            for e in range(extra[1].shape[0]):
                total += score_ref[:, e : e + 1] * router_ref[e : e + 1, :].astype(F32)
        out_ref[...] = total.astype(BF)

    in_specs = (
        [pl.BlockSpec((tokens, slots), lambda j: (0, 0))] * top
        + [pl.BlockSpec(factors.shape, lambda j: (0, 0))]
        + [pl.BlockSpec((CAP, block), lambda j: (0, j)) for _ in range(pieces)]
        + [pl.BlockSpec((tokens, block), lambda j: (0, j))]
    )
    operands = list(picks) + [factors] + list(returned) + [rows]
    if extra is not None:
        in_specs += [
            pl.BlockSpec(extra[0].shape, lambda j: (0, 0)),
            pl.BlockSpec((extra[1].shape[0], block), lambda j: (0, j)),
        ]
        operands += list(extra)
    return pl.pallas_call(
        body,
        grid=(features // block,),
        in_specs=in_specs,
        out_specs=pl.BlockSpec((tokens, block), lambda j: (0, j)),
        out_shape=jax.ShapeDtypeStruct((tokens, features), BF),
        compiler_params=params(1),
        name=name,
    )(*operands)


def shards(
    forward_rows,
    forward_ids,
    backward_rows,
    backward_ids,
    backward_grad,
    backward_stash,
    router,
    w_gate,
    w_up,
    w_down,
):
    fwd_rows, fwd_ids = forward_rows[0], forward_ids[0]
    bwd_rows, bwd_ids, bwd_grad = backward_rows[0], backward_ids[0], backward_grad[0]
    router_rows = router[0]
    gate_w, up_w, down_w = w_gate[0, 0], w_up[0, 0], w_down[0, 0]
    members = lax.axis_size("expert")
    experts, features = router_rows.shape
    hidden = down_w.shape[0]
    tokens, top = fwd_ids.shape
    slots = experts * CAP
    index = lax.axis_index("expert")
    level = index // 4
    core = jnp.reshape(index % 2, (1,))
    chip = jnp.reshape(level % 2 * 2 + index // 2 % 2, (1,))
    slot_axis = jnp.arange(slots, dtype=jnp.int32)

    joined_w = jnp.concatenate([gate_w, up_w], axis=1)

    slot_f = route_plan(fwd_ids, experts, level)
    slot_b = route_plan(bwd_ids, experts, level)
    select_f = jnp.sum(slot_axis[:, None, None] == slot_f[None], axis=2).astype(BF)
    select_b = jnp.sum(slot_axis[:, None, None] == slot_b[None], axis=2).astype(BF)
    pairs_b = (slot_axis[:, None] == slot_b.reshape(1, tokens * top)).astype(BF)
    stash = backward_stash[0].reshape(tokens * top, 2 * backward_stash.shape[-1])
    sent = pack(core, select_f, select_b, pairs_b, fwd_rows, bwd_grad, stash, hidden)
    near, far = sent

    first = hopped(far, 2)
    down_y, down_z = exchanged(down_w, 2), exchanged(down_w, 4)
    joined_y, joined_z = exchanged(joined_w, 2), exchanged(joined_w, 4)
    first, down_y, joined_z, down_z, joined_y = lax.optimization_barrier(
        (first, down_y, joined_z, down_z, joined_y)
    )

    own_1 = jnp.concatenate([near[:CAP], first[:CAP]], axis=0)
    own_2 = hopped(jnp.concatenate([near[CAP:], first[CAP:]], axis=0), 1)
    other_1 = exchanged(own_1, 1)
    down_d, joined_d = exchanged(down_y, 4), exchanged(joined_z, 2)
    own_2, other_1, down_d, joined_d = lax.optimization_barrier((own_2, other_1, down_d, joined_d))
    parts = [own_1, own_2, other_1, exchanged(own_2, 1)]
    downs = [down_w, down_y, down_z, down_d]
    joins = [joined_w, joined_y, joined_z, joined_d]

    d_joined, inner = backward_first(chip, parts, downs)
    keep, give = backward_second(d_joined, joins)
    swapped = exchanged(give, 1)
    inner = inner[:slots, 0] + exchanged(inner[slots:, 0], 1)
    inner = jnp.pad(inner.reshape(experts, 1, CAP), ((0, 0), (0, 0), (0, features - CAP))).astype(BF)
    is_inner = lax.broadcasted_iota(jnp.int32, (CAP, 1), 0) == USED
    pieces = [
        jnp.where(is_inner, inner[place], rows)
        for place, rows in zip((0, 2, 1, 3), merged(keep, swapped))
    ]
    parts, pieces = lax.optimization_barrier((parts, pieces))
    back_b = [to_source(rows, k) for k, rows in enumerate(pieces)]
    hidden_f = forward_first(parts, joins)
    keep, give = forward_second(hidden_f, downs)
    swapped = exchanged(give, 1)
    back_f = [to_source(rows, k) for k, rows in enumerate(merged(keep, swapped))]

    one_hot_b, probs_b, total_b = gate_terms(bwd_rows, bwd_ids, router_rows)
    share_b = probs_b / total_b
    scale_b = (ROUTE_SCALE * share_b).astype(BF).astype(F32)
    picks_b = [(slot_b[:, k : k + 1] == slot_axis[None, :]).astype(BF) for k in range(top)]
    inner_all = jnp.concatenate([rows[USED : USED + 1, :CAP] for rows in back_b], axis=1)
    inner_all = inner_all.astype(F32)
    inner_sum = jnp.stack(
        [jnp.sum(picks_b[k].astype(F32) * inner_all, axis=1) for k in range(top)], axis=1
    )
    d_logit = (
        ROUTE_SCALE
        / total_b
        * (inner_sum - jnp.sum(share_b * inner_sum, axis=1, keepdims=True))
        * probs_b
        * (1.0 - probs_b)
    )
    score_grad = jnp.sum(one_hot_b * d_logit[:, :, None], axis=1)
    router_total = jnp.dot(score_grad.T, bwd_rows.astype(F32), precision=lax.Precision.HIGHEST)
    router_total = router_total * (1.0 / (tokens * members))
    shares = jnp.transpose(router_total.reshape(experts, members, features // members), (1, 0, 2))
    shares = all_to_all(shares)
    shares = all_to_all(jnp.broadcast_to(jnp.sum(shares, axis=0)[None], shares.shape))
    router_total = jnp.transpose(shares, (1, 0, 2)).reshape(experts, features)
    back_f, router_total = lax.optimization_barrier((back_f, router_total))
    extra = (score_grad, router_rows)
    input_grad = combine(picks_b, scale_b, back_b, bwd_grad, extra, "combine_backward")
    backward_out_rows = shifted(input_grad, "pipe", -1)

    one_hot_f, probs_f, total_f = gate_terms(fwd_rows, fwd_ids, router_rows)
    weights_f = ROUTE_SCALE * probs_f / total_f
    picks_f = [(slot_f[:, k : k + 1] == slot_axis[None, :]).astype(BF) for k in range(top)]
    layer_out = combine(picks_f, weights_f, back_f, fwd_rows, None, "combine_forward")
    forward_out_rows = shifted(layer_out, "pipe", 1)
    return (forward_out_rows[None], backward_out_rows[None], router_total[None])


def solution(mesh):
    return jax.shard_map(
        shards,
        mesh=mesh,
        in_specs=(
            P("pipe", "expert", None),
            P("pipe", "expert", None),
            P("pipe", "expert", None),
            P("pipe", "expert", None),
            P("pipe", "expert", None),
            P("pipe", "expert", None, None, None),
            P("pipe", None, None),
            P("pipe", "expert", None, None),
            P("pipe", "expert", None, None),
            P("pipe", "expert", None, None),
        ),
        out_specs=(P("pipe", "expert", None), P("pipe", "expert", None), P("pipe", None, None)),
        check_vma=False,
    )
```

```python
import jax
import jax.numpy as jnp
from jax import lax
from jax.experimental import pallas as pl
from jax.experimental.pallas import tpu as pltpu
from jax.sharding import PartitionSpec as P

CAP = 40
ROUTE_SCALE = 2.5
BF = jnp.bfloat16
F32 = jnp.float32
USED = 36
VMEM_BYTES = 48 * 1024 * 1024


def params(steps):
    return pltpu.CompilerParams(
        dimension_semantics=("arbitrary",) * steps, vmem_limit_bytes=VMEM_BYTES
    )


def shifted(block, axis, distance):
    devices = range(lax.axis_size(axis))
    route = [((i - distance) % len(devices), i) for i in devices]
    return lax.ppermute(block, axis, route)


def exchanged(block, mask):
    route = [(i, i ^ mask) for i in range(lax.axis_size("expert"))]
    return lax.ppermute(block, "expert", route)


def all_to_all(block):
    return lax.all_to_all(block, "expert", split_axis=0, concat_axis=0, tiled=True)


def piece_route(piece):
    members = lax.axis_size("expert")
    step = (0, 2, -1, -3)[piece]
    return [(i, (i + 4 * (step if i // 4 % 2 == 0 else -step)) % members) for i in range(members)]


def hopped(block, piece):
    return lax.ppermute(block, "expert", piece_route(piece))


def to_source(block, piece):
    if not piece:
        return block
    return lax.ppermute(block, "expert", [(b, a) for a, b in piece_route(piece)])


def gate_terms(tok_rows, ids, router_rows):
    experts = router_rows.shape[0]
    logits = lax.dot_general(
        tok_rows, router_rows, (((1,), (1,)), ((), ())), preferred_element_type=F32
    )
    one_hot = (ids[:, :, None] == jnp.arange(experts, dtype=jnp.int32)[None, None, :]).astype(F32)
    probs_m = jax.nn.sigmoid(jnp.sum(one_hot * logits[:, None, :], axis=2))
    total_m = jnp.sum(probs_m, axis=1, keepdims=True)
    return one_hot, probs_m, total_m


def route_plan(ids, experts, level):
    tokens, top = ids.shape
    flat_ids = ids.reshape(tokens * top)
    one_hot = (flat_ids[:, None] == jnp.arange(experts, dtype=jnp.int32)[None, :]).astype(jnp.int32)
    before = jnp.cumsum(one_hot, axis=0) - one_hot
    rank = jnp.sum(before * one_hot, axis=1)
    ahead = flat_ids - level // 2
    ahead = jnp.where(level % 2 == 0, ahead, -ahead) % experts
    piece = jnp.where(ahead == 2, 3, jnp.where(ahead == 3, 2, ahead))
    return (piece * CAP + rank).reshape(tokens, top)


def pack(core, select_f, select_b, select_pairs, rows_f, rows_b, stash, hidden):
    tokens, features = rows_f.shape
    slots, pairs = select_pairs.shape
    lanes = stash.shape[1]
    quarter = lanes // 4
    chips = quarter // hidden
    total = 2 * features + lanes
    block = total // 4

    def body(core_ref, f_ref, b_ref, pairs_ref, rows_f_ref, rows_b_ref, stash_ref, *out_refs):
        def spread(select_ref, source, at):
            got = jnp.dot(select_ref[...], source, preferred_element_type=F32)
            for k in range(2):
                half = got[k * slots // 2 : (k + 1) * slots // 2]
                out_refs[k][:, at : at + source.shape[1]] = half.astype(BF)

        def fill(step):
            first, last = step * block, (step + 1) * block
            for select_ref, ref, start in ((f_ref, rows_f_ref, 0), (b_ref, rows_b_ref, features)):
                low, high = max(first, start), min(last, start + features)
                if low < high:
                    spread(select_ref, ref[:, low - start : high - start], low - first)
            for place in range(4 * chips):
                at = 2 * features + place * hidden
                if first <= at < last:
                    owner = (core_ref[0] + 1 + place // (2 * chips)) % 2
                    part, chip = place // chips % 2, place % chips
                    start = part * 2 * quarter + (2 * chip + owner) * hidden
                    source = stash_ref[:, pl.ds(pl.multiple_of(start, hidden), hidden)]
                    spread(pairs_ref, source, at - first)

        for step in range(4):
            pl.when(pl.program_id(0) == step)(lambda step=step: fill(step))

    def whole(array):
        return pl.BlockSpec(array.shape, lambda j: (0, 0))

    return pl.pallas_call(
        body,
        grid=(4,),
        in_specs=[pl.BlockSpec(memory_space=pltpu.SMEM)]
        + [whole(a) for a in (select_f, select_b, select_pairs, rows_f, rows_b, stash)],
        out_specs=[pl.BlockSpec((slots // 2, block), lambda j: (0, j))] * 2,
        out_shape=[jax.ShapeDtypeStruct((slots // 2, total), BF)] * 2,
        compiler_params=params(1),
        name="pack",
    )(core, select_f, select_b, select_pairs, rows_f, rows_b, stash)


def contract(left, right, right_dim):
    return lax.dot_general(left, right, (((1,), (right_dim,)), ((), ())), preferred_element_type=F32)


def silu_slope(pre_act):
    sigmoid_v = jax.nn.sigmoid(pre_act)
    return sigmoid_v * (1.0 + pre_act * (1.0 - sigmoid_v))


def backward_first(chip, parts, downs):
    rows = parts[0].shape[0]
    chips, count = len(downs), len(parts)
    hidden, features = downs[0].shape
    block = 1792
    steps = features // block
    wide = 2 * chips * hidden

    def body(chip_ref, *refs):
        row_refs, stash_refs, refs = refs[:count], refs[count : 2 * count], refs[2 * count :]
        w_refs, (d_ref, inner_ref, total) = refs[:chips], refs[chips:]
        step = pl.program_id(0)
        left = jnp.concatenate([ref[...] for ref in row_refs], axis=0)
        right = jnp.concatenate([ref[...] for ref in w_refs], axis=0)
        got = contract(left, right, 1)

        @pl.when(step == 0)
        def _():
            total[...] = got

        @pl.when(step > 0)
        def _():
            total[...] += got

        @pl.when(step == steps - 1)
        def _():
            for part, stash_ref in enumerate(stash_refs):
                place = slice(part * rows, (part + 1) * rows)
                products = jnp.zeros((rows, hidden), F32)
                for s in range(chips):
                    start = (chip_ref[0] ^ s) * hidden
                    pre_gate = stash_ref[:, pl.ds(pl.multiple_of(start, hidden), hidden)].astype(F32)
                    start = start + chips * hidden
                    pre_up = stash_ref[:, pl.ds(pl.multiple_of(start, hidden), hidden)].astype(F32)
                    raw = total[place, s * hidden : (s + 1) * hidden]
                    sigmoid_v = jax.nn.sigmoid(pre_gate)
                    activated = pre_gate * sigmoid_v
                    slope = sigmoid_v * (1.0 + pre_gate * (1.0 - sigmoid_v))
                    hidden_b = (activated * pre_up).astype(BF).astype(F32)
                    products += hidden_b * raw
                    at = 2 * s * hidden
                    d_ref[place, at : at + hidden] = (raw * pre_up * slope).astype(BF)
                    d_ref[place, at + hidden : at + 2 * hidden] = (raw * activated).astype(BF)
                high = products.astype(BF)
                low = (products - high.astype(F32)).astype(BF)
                ones = jnp.ones((8, hidden), BF)
                for k in range(rows // CAP):
                    piece = slice(k * CAP, (k + 1) * CAP)
                    inner = contract(ones, high[piece], 1) + contract(ones, low[piece], 1)
                    inner = jnp.pad(inner, ((0, 0), (0, hidden - CAP)))
                    at = 8 * (part * rows // CAP + k)
                    inner_ref[at : at + 8, :] = inner

    return pl.pallas_call(
        body,
        grid=(steps,),
        in_specs=[pl.BlockSpec(memory_space=pltpu.SMEM)]
        + [pl.BlockSpec((rows, block), lambda j: (0, steps + j))] * count
        + [pl.BlockSpec((rows, wide), lambda j: (0, 2 * features // wide + 1))] * (count // 2)
        + [pl.BlockSpec((rows, wide), lambda j: (0, 2 * features // wide))] * (count // 2)
        + [pl.BlockSpec((hidden, block), lambda j: (0, j))] * chips,
        out_specs=[
            pl.BlockSpec((count * rows, 2 * chips * hidden), lambda j: (0, 0)),
            pl.BlockSpec((count * rows // CAP * 8, hidden), lambda j: (0, 0)),
        ],
        out_shape=[
            jax.ShapeDtypeStruct((count * rows, 2 * chips * hidden), BF),
            jax.ShapeDtypeStruct((count * rows // CAP * 8, hidden), F32),
        ],
        scratch_shapes=[pltpu.VMEM((count * rows, chips * hidden), F32)],
        compiler_params=params(1),
        name="backward_first",
    )(chip, *parts, *parts, *downs)


def backward_second(d_joined, inner, weights):
    rows = d_joined.shape[0] // 2
    features, joined = weights[0].shape
    chips = len(weights)
    block = 1792
    lanes = inner.shape[1]

    def body(d_ref, inner_ref, *refs):
        out_refs = refs[chips:]
        right = jnp.concatenate([ref[...] for ref in refs[:chips]], axis=1)
        got = contract(d_ref[...], right, 1)
        for half, out_ref in enumerate(out_refs):
            out_ref[...] = got[half * rows : (half + 1) * rows].astype(BF)

        @pl.when(pl.program_id(0) == 0)
        def _():
            used = lax.broadcasted_iota(jnp.int32, (CAP, lanes), 0) == USED
            for half, out_ref in enumerate(out_refs):
                pieces = []
                for k in range(half * rows // CAP, (half + 1) * rows // CAP):
                    piece = got[k * CAP : (k + 1) * CAP, :lanes]
                    pieces.append(jnp.where(used, inner_ref[8 * k : 8 * k + 1, :], piece))
                out_ref[:, :lanes] = jnp.concatenate(pieces, axis=0).astype(BF)

    return pl.pallas_call(
        body,
        grid=(features // block,),
        in_specs=[pl.BlockSpec(a.shape, lambda j: (0, 0)) for a in (d_joined, inner)]
        + [pl.BlockSpec((block, joined), lambda j: (j, 0))] * chips,
        out_specs=[pl.BlockSpec((rows, block), lambda j: (0, j))] * 2,
        out_shape=[jax.ShapeDtypeStruct((rows, features), BF)] * 2,
        compiler_params=params(1),
        name="backward_second",
    )(d_joined, inner, *weights)


def forward_first(parts, weights):
    rows, count = parts[0].shape[0], len(parts)
    features, joined = weights[0].shape
    chips = len(weights)
    hidden = joined // 2
    block = 1792
    steps = features // block

    def body(*refs):
        row_refs, refs = refs[:count], refs[count:]
        out_ref, total = refs[chips:]
        step = pl.program_id(0)
        right = jnp.concatenate([ref[...] for ref in refs[:chips]], axis=1)
        left = jnp.concatenate([ref[...] for ref in row_refs], axis=0)
        got = contract(left, right, 0)

        @pl.when(step == 0)
        def _():
            total[...] = got

        @pl.when(step > 0)
        def _():
            total[...] += got

        @pl.when(step == steps - 1)
        def _():
            for s in range(chips):
                at = 2 * s * hidden
                gate = total[:, at : at + hidden]
                up = total[:, at + hidden : at + 2 * hidden]
                out_ref[:, s * hidden : (s + 1) * hidden] = (jax.nn.silu(gate) * up).astype(BF)

    return pl.pallas_call(
        body,
        grid=(steps,),
        in_specs=[pl.BlockSpec((rows, block), lambda j: (0, j))] * count
        + [pl.BlockSpec((block, joined), lambda j: (j, 0))] * chips,
        out_specs=pl.BlockSpec((count * rows, chips * hidden), lambda j: (0, 0)),
        out_shape=jax.ShapeDtypeStruct((count * rows, chips * hidden), BF),
        scratch_shapes=[pltpu.VMEM((count * rows, chips * joined), F32)],
        compiler_params=params(1),
        name="forward_first",
    )(*parts, *weights)


def forward_second(hidden_f, downs):
    rows = hidden_f.shape[0] // 2
    hidden, features = downs[0].shape
    chips = len(downs)
    block = 1792

    def body(hidden_ref, *refs):
        keep_ref, give_ref = refs[chips:]
        right = jnp.concatenate([ref[...] for ref in refs[:chips]], axis=0)
        got = contract(hidden_ref[...], right, 0)
        keep_ref[...] = got[:rows].astype(BF)
        give_ref[...] = got[rows:].astype(BF)

    return pl.pallas_call(
        body,
        grid=(features // block,),
        in_specs=[pl.BlockSpec(hidden_f.shape, lambda j: (0, 0))]
        + [pl.BlockSpec((hidden, block), lambda j: (0, j))] * chips,
        out_specs=[pl.BlockSpec((rows, block), lambda j: (0, j))] * 2,
        out_shape=[jax.ShapeDtypeStruct((rows, features), BF)] * 2,
        compiler_params=params(1),
        name="forward_second",
    )(hidden_f, *downs)


def merged(keep, swapped):
    total = (keep.astype(F32) + swapped.astype(F32)).astype(BF)
    return [total[place * CAP : (place + 1) * CAP] for place in (0, 2, 1, 3)]


def combine(picks, factors, returned, rows, extra, name):
    tokens = rows.shape[0]
    features = returned[0].shape[1]
    block = 3584
    top, pieces = len(picks), len(returned)
    slots = picks[0].shape[1]

    def body(*refs):
        pick_refs, factor_ref, refs = refs[:top], refs[top], refs[top + 1 :]
        back_refs, rows_ref, refs = refs[:pieces], refs[pieces], refs[pieces + 1 :]
        out_ref = refs[-1]
        back = jnp.concatenate([ref[...].astype(F32) for ref in back_refs], axis=0).astype(BF)
        total = rows_ref[...].astype(F32)
        for k in range(top):
            picked = jnp.dot(pick_refs[k][...], back, preferred_element_type=F32)
            total += factor_ref[:, k : k + 1] * picked
        if extra is not None:
            score_ref, router_ref = refs[:2]
            for e in range(extra[1].shape[0]):
                total += score_ref[:, e : e + 1] * router_ref[e : e + 1, :].astype(F32)
        out_ref[...] = total.astype(BF)

    in_specs = (
        [pl.BlockSpec((tokens, slots), lambda j: (0, 0))] * top
        + [pl.BlockSpec(factors.shape, lambda j: (0, 0))]
        + [pl.BlockSpec((CAP, block), lambda j: (0, j)) for _ in range(pieces)]
        + [pl.BlockSpec((tokens, block), lambda j: (0, j))]
    )
    operands = list(picks) + [factors] + list(returned) + [rows]
    if extra is not None:
        in_specs += [
            pl.BlockSpec(extra[0].shape, lambda j: (0, 0)),
            pl.BlockSpec((extra[1].shape[0], block), lambda j: (0, j)),
        ]
        operands += list(extra)
    return pl.pallas_call(
        body,
        grid=(features // block,),
        in_specs=in_specs,
        out_specs=pl.BlockSpec((tokens, block), lambda j: (0, j)),
        out_shape=jax.ShapeDtypeStruct((tokens, features), BF),
        compiler_params=params(1),
        name=name,
    )(*operands)


def shards(
    forward_rows,
    forward_ids,
    backward_rows,
    backward_ids,
    backward_grad,
    backward_stash,
    router,
    w_gate,
    w_up,
    w_down,
):
    fwd_rows, fwd_ids = forward_rows[0], forward_ids[0]
    bwd_rows, bwd_ids, bwd_grad = backward_rows[0], backward_ids[0], backward_grad[0]
    router_rows = router[0]
    gate_w, up_w, down_w = w_gate[0, 0], w_up[0, 0], w_down[0, 0]
    members = lax.axis_size("expert")
    experts, features = router_rows.shape
    hidden = down_w.shape[0]
    tokens, top = fwd_ids.shape
    slots = experts * CAP
    index = lax.axis_index("expert")
    level = index // 4
    core = jnp.reshape(index % 2, (1,))
    chip = jnp.reshape(level % 2 * 2 + index // 2 % 2, (1,))
    slot_axis = jnp.arange(slots, dtype=jnp.int32)

    joined_w = jnp.concatenate([gate_w, up_w], axis=1)

    slot_f = route_plan(fwd_ids, experts, level)
    slot_b = route_plan(bwd_ids, experts, level)
    select_f = jnp.sum(slot_axis[:, None, None] == slot_f[None], axis=2).astype(BF)
    select_b = jnp.sum(slot_axis[:, None, None] == slot_b[None], axis=2).astype(BF)
    pairs_b = (slot_axis[:, None] == slot_b.reshape(1, tokens * top)).astype(BF)
    stash = backward_stash[0].reshape(tokens * top, 2 * backward_stash.shape[-1])
    sent = pack(core, select_f, select_b, pairs_b, fwd_rows, bwd_grad, stash, hidden)
    near, far = sent

    first = hopped(far, 2)
    down_y, down_z = exchanged(down_w, 2), exchanged(down_w, 4)
    joined_y, joined_z = exchanged(joined_w, 2), exchanged(joined_w, 4)
    first, down_y, joined_z, down_z, joined_y = lax.optimization_barrier(
        (first, down_y, joined_z, down_z, joined_y)
    )

    own_1 = jnp.concatenate([near[:CAP], first[:CAP]], axis=0)
    own_2 = hopped(jnp.concatenate([near[CAP:], first[CAP:]], axis=0), 1)
    other_1 = exchanged(own_1, 1)
    cut = hidden // 3 // 16 * 16
    down_d = [exchanged(down_z[:cut], 2), exchanged(down_y[cut:], 4)]
    joined_d = exchanged(joined_z, 2)
    own_2, other_1, down_d, joined_d = lax.optimization_barrier((own_2, other_1, down_d, joined_d))
    parts = [own_1, own_2, other_1, exchanged(own_2, 1)]
    downs = [down_w, down_y, down_z, jnp.concatenate(down_d, axis=0)]
    joins = [joined_w, joined_y, joined_z, joined_d]

    d_joined, inner = backward_first(chip, parts, downs)
    keep, give = backward_second(d_joined, inner, joins)
    pieces = merged(keep, exchanged(give, 1))
    parts, pieces = lax.optimization_barrier((parts, pieces))
    back_b = [to_source(rows, k) for k, rows in enumerate(pieces)]
    hidden_f = forward_first(parts, joins)
    keep, give = forward_second(hidden_f, downs)
    swapped = exchanged(give, 1)
    back_f = [to_source(rows, k) for k, rows in enumerate(merged(keep, swapped))]

    back_b = lax.optimization_barrier(back_b)
    one_hot_b, probs_b, total_b = gate_terms(bwd_rows, bwd_ids, router_rows)
    share_b = probs_b / total_b
    scale_b = (ROUTE_SCALE * share_b).astype(BF).astype(F32)
    picks_b = [(slot_b[:, k : k + 1] == slot_axis[None, :]).astype(BF) for k in range(top)]
    inner_all = jnp.concatenate([rows[USED : USED + 1, :CAP] for rows in back_b], axis=1)
    inner_all = inner_all.astype(F32)
    inner_sum = jnp.stack(
        [jnp.sum(picks_b[k].astype(F32) * inner_all, axis=1) for k in range(top)], axis=1
    )
    d_logit = (
        ROUTE_SCALE
        / total_b
        * (inner_sum - jnp.sum(share_b * inner_sum, axis=1, keepdims=True))
        * probs_b
        * (1.0 - probs_b)
    )
    score_grad = jnp.sum(one_hot_b * d_logit[:, :, None], axis=1)
    router_total = jnp.dot(score_grad.T, bwd_rows.astype(F32), precision=lax.Precision.HIGHEST)
    router_total = router_total * (1.0 / (tokens * members))
    shares = jnp.transpose(router_total.reshape(experts, members, features // members), (1, 0, 2))
    shares = all_to_all(shares)
    extra = (score_grad, router_rows)
    input_grad = combine(picks_b, scale_b, back_b, bwd_grad, extra, "combine_backward")
    backward_out_rows = shifted(input_grad, "pipe", -1)
    back_f, _ = lax.optimization_barrier((back_f, input_grad))

    one_hot_f, probs_f, total_f = gate_terms(fwd_rows, fwd_ids, router_rows)
    weights_f = ROUTE_SCALE * probs_f / total_f
    picks_f = [(slot_f[:, k : k + 1] == slot_axis[None, :]).astype(BF) for k in range(top)]
    layer_out = combine(picks_f, weights_f, back_f, fwd_rows, None, "combine_forward")
    shares, layer_out = lax.optimization_barrier((shares, layer_out))
    shares = all_to_all(jnp.broadcast_to(jnp.sum(shares, axis=0)[None], shares.shape))
    router_total = jnp.transpose(shares, (1, 0, 2)).reshape(experts, features)
    forward_out_rows = shifted(layer_out, "pipe", 1)
    return (forward_out_rows[None], backward_out_rows[None], router_total[None])


def solution(mesh):
    return jax.shard_map(
        shards,
        mesh=mesh,
        in_specs=(
            P("pipe", "expert", None),
            P("pipe", "expert", None),
            P("pipe", "expert", None),
            P("pipe", "expert", None),
            P("pipe", "expert", None),
            P("pipe", "expert", None, None, None),
            P("pipe", None, None),
            P("pipe", "expert", None, None),
            P("pipe", "expert", None, None),
            P("pipe", "expert", None, None),
        ),
        out_specs=(P("pipe", "expert", None), P("pipe", "expert", None), P("pipe", None, None)),
        check_vma=False,
    )
```

```python
import jax
import jax.numpy as jnp
from jax import lax
from jax.experimental import pallas as pl
from jax.experimental.pallas import tpu as pltpu
from jax.sharding import PartitionSpec as P

CAP = 40
ROUTE_SCALE = 2.5
BF = jnp.bfloat16
F32 = jnp.float32
USED = 36
VMEM_BYTES = 48 * 1024 * 1024


def params(steps):
    return pltpu.CompilerParams(
        dimension_semantics=("arbitrary",) * steps, vmem_limit_bytes=VMEM_BYTES
    )


def shifted(block, axis, distance):
    devices = range(lax.axis_size(axis))
    route = [((i - distance) % len(devices), i) for i in devices]
    return lax.ppermute(block, axis, route)


def exchanged(block, mask):
    route = [(i, i ^ mask) for i in range(lax.axis_size("expert"))]
    return lax.ppermute(block, "expert", route)


def all_to_all(block):
    return lax.all_to_all(block, "expert", split_axis=0, concat_axis=0, tiled=True)


def piece_route(piece):
    members = lax.axis_size("expert")
    step = (0, 2, -1, -3)[piece]
    return [(i, (i + 4 * (step if i // 4 % 2 == 0 else -step)) % members) for i in range(members)]


def hopped(block, piece):
    return lax.ppermute(block, "expert", piece_route(piece))


def to_source(block, piece):
    if not piece:
        return block
    return lax.ppermute(block, "expert", [(b, a) for a, b in piece_route(piece)])


def to_next(block, piece):
    sections, members = lax.axis_size("pipe"), lax.axis_size("expert")
    route = [
        (p * members + b, (p + 1) % sections * members + a)
        for p in range(sections)
        for a, b in piece_route(piece)
    ]
    return lax.ppermute(block, ("pipe", "expert"), route)


def gate_terms(tok_rows, ids, router_rows):
    experts = router_rows.shape[0]
    logits = lax.dot_general(
        tok_rows, router_rows, (((1,), (1,)), ((), ())), preferred_element_type=F32
    )
    one_hot = (ids[:, :, None] == jnp.arange(experts, dtype=jnp.int32)[None, None, :]).astype(F32)
    probs_m = jax.nn.sigmoid(jnp.sum(one_hot * logits[:, None, :], axis=2))
    total_m = jnp.sum(probs_m, axis=1, keepdims=True)
    return one_hot, probs_m, total_m


def route_plan(ids, experts, level):
    tokens, top = ids.shape
    flat_ids = ids.reshape(tokens * top)
    one_hot = (flat_ids[:, None] == jnp.arange(experts, dtype=jnp.int32)[None, :]).astype(jnp.int32)
    before = jnp.cumsum(one_hot, axis=0) - one_hot
    rank = jnp.sum(before * one_hot, axis=1)
    ahead = flat_ids - level // 2
    ahead = jnp.where(level % 2 == 0, ahead, -ahead) % experts
    piece = jnp.where(ahead == 2, 3, jnp.where(ahead == 3, 2, ahead))
    return (piece * CAP + rank).reshape(tokens, top)


def pack(core, select_f, select_b, select_pairs, rows_f, rows_b, stash, hidden):
    tokens, features = rows_f.shape
    slots, pairs = select_pairs.shape
    lanes = stash.shape[1]
    quarter = lanes // 4
    chips = quarter // hidden
    total = 2 * features + lanes
    block = total // 4

    def body(core_ref, f_ref, b_ref, pairs_ref, rows_f_ref, rows_b_ref, stash_ref, *out_refs):
        def spread(select_ref, source, at):
            got = jnp.dot(select_ref[...], source, preferred_element_type=F32)
            for k in range(2):
                half = got[k * slots // 2 : (k + 1) * slots // 2]
                out_refs[k][:, at : at + source.shape[1]] = half.astype(BF)

        def fill(step):
            first, last = step * block, (step + 1) * block
            for select_ref, ref, start in ((f_ref, rows_f_ref, 0), (b_ref, rows_b_ref, features)):
                low, high = max(first, start), min(last, start + features)
                if low < high:
                    spread(select_ref, ref[:, low - start : high - start], low - first)
            for place in range(4 * chips):
                at = 2 * features + place * hidden
                if first <= at < last:
                    owner = (core_ref[0] + 1 + place // (2 * chips)) % 2
                    part, chip = place // chips % 2, place % chips
                    start = part * 2 * quarter + (2 * chip + owner) * hidden
                    source = stash_ref[:, pl.ds(pl.multiple_of(start, hidden), hidden)]
                    spread(pairs_ref, source, at - first)

        for step in range(4):
            pl.when(pl.program_id(0) == step)(lambda step=step: fill(step))

    def whole(array):
        return pl.BlockSpec(array.shape, lambda j: (0, 0))

    return pl.pallas_call(
        body,
        grid=(4,),
        in_specs=[pl.BlockSpec(memory_space=pltpu.SMEM)]
        + [whole(a) for a in (select_f, select_b, select_pairs, rows_f, rows_b, stash)],
        out_specs=[pl.BlockSpec((slots // 2, block), lambda j: (0, j))] * 2,
        out_shape=[jax.ShapeDtypeStruct((slots // 2, total), BF)] * 2,
        compiler_params=params(1),
        name="pack",
    )(core, select_f, select_b, select_pairs, rows_f, rows_b, stash)


def contract(left, right, right_dim):
    return lax.dot_general(left, right, (((1,), (right_dim,)), ((), ())), preferred_element_type=F32)


def silu_slope(pre_act):
    sigmoid_v = jax.nn.sigmoid(pre_act)
    return sigmoid_v * (1.0 + pre_act * (1.0 - sigmoid_v))


def backward_first(chip, parts, downs):
    rows = parts[0].shape[0]
    chips, count = len(downs), len(parts)
    hidden, features = downs[0].shape
    block = 1792
    steps = features // block
    wide = 2 * chips * hidden

    def body(chip_ref, *refs):
        row_refs, stash_refs, refs = refs[:count], refs[count : 2 * count], refs[2 * count :]
        w_refs, (d_ref, inner_ref, total) = refs[:chips], refs[chips:]
        step = pl.program_id(0)
        left = jnp.concatenate([ref[...] for ref in row_refs], axis=0)
        right = jnp.concatenate([ref[...] for ref in w_refs], axis=0)
        got = contract(left, right, 1)

        @pl.when(step == 0)
        def _():
            total[...] = got

        @pl.when(step > 0)
        def _():
            total[...] += got

        @pl.when(step == steps - 1)
        def _():
            for part, stash_ref in enumerate(stash_refs):
                place = slice(part * rows, (part + 1) * rows)
                products = jnp.zeros((rows, hidden), F32)
                for s in range(chips):
                    start = (chip_ref[0] ^ s) * hidden
                    pre_gate = stash_ref[:, pl.ds(pl.multiple_of(start, hidden), hidden)].astype(F32)
                    start = start + chips * hidden
                    pre_up = stash_ref[:, pl.ds(pl.multiple_of(start, hidden), hidden)].astype(F32)
                    raw = total[place, s * hidden : (s + 1) * hidden]
                    sigmoid_v = jax.nn.sigmoid(pre_gate)
                    activated = pre_gate * sigmoid_v
                    slope = sigmoid_v * (1.0 + pre_gate * (1.0 - sigmoid_v))
                    hidden_b = (activated * pre_up).astype(BF).astype(F32)
                    products += hidden_b * raw
                    at = 2 * s * hidden
                    d_ref[place, at : at + hidden] = (raw * pre_up * slope).astype(BF)
                    d_ref[place, at + hidden : at + 2 * hidden] = (raw * activated).astype(BF)
                high = products.astype(BF)
                low = (products - high.astype(F32)).astype(BF)
                ones = jnp.ones((8, hidden), BF)
                for k in range(rows // CAP):
                    piece = slice(k * CAP, (k + 1) * CAP)
                    inner = contract(ones, high[piece], 1) + contract(ones, low[piece], 1)
                    inner = jnp.pad(inner, ((0, 0), (0, hidden - CAP)))
                    at = 8 * (part * rows // CAP + k)
                    inner_ref[at : at + 8, :] = inner

    return pl.pallas_call(
        body,
        grid=(steps,),
        in_specs=[pl.BlockSpec(memory_space=pltpu.SMEM)]
        + [pl.BlockSpec((rows, block), lambda j: (0, steps + j))] * count
        + [pl.BlockSpec((rows, wide), lambda j: (0, 2 * features // wide + 1))] * (count // 2)
        + [pl.BlockSpec((rows, wide), lambda j: (0, 2 * features // wide))] * (count // 2)
        + [pl.BlockSpec((hidden, block), lambda j: (0, j))] * chips,
        out_specs=[
            pl.BlockSpec((count * rows, 2 * chips * hidden), lambda j: (0, 0)),
            pl.BlockSpec((count * rows // CAP * 8, hidden), lambda j: (0, 0)),
        ],
        out_shape=[
            jax.ShapeDtypeStruct((count * rows, 2 * chips * hidden), BF),
            jax.ShapeDtypeStruct((count * rows // CAP * 8, hidden), F32),
        ],
        scratch_shapes=[pltpu.VMEM((count * rows, chips * hidden), F32)],
        compiler_params=params(1),
        name="backward_first",
    )(chip, *parts, *parts, *downs)


def backward_second(d_joined, inner, weights):
    rows = d_joined.shape[0] // 2
    features, joined = weights[0].shape
    chips = len(weights)
    block = 1792
    lanes = inner.shape[1]

    def body(d_ref, inner_ref, *refs):
        out_refs = refs[chips:]
        right = jnp.concatenate([ref[...] for ref in refs[:chips]], axis=1)
        got = contract(d_ref[...], right, 1)
        for half, out_ref in enumerate(out_refs):
            out_ref[...] = got[half * rows : (half + 1) * rows].astype(BF)

        @pl.when(pl.program_id(0) == 0)
        def _():
            used = lax.broadcasted_iota(jnp.int32, (CAP, lanes), 0) == USED
            for half, out_ref in enumerate(out_refs):
                pieces = []
                for k in range(half * rows // CAP, (half + 1) * rows // CAP):
                    piece = got[k * CAP : (k + 1) * CAP, :lanes]
                    pieces.append(jnp.where(used, inner_ref[8 * k : 8 * k + 1, :], piece))
                out_ref[:, :lanes] = jnp.concatenate(pieces, axis=0).astype(BF)

    return pl.pallas_call(
        body,
        grid=(features // block,),
        in_specs=[pl.BlockSpec(a.shape, lambda j: (0, 0)) for a in (d_joined, inner)]
        + [pl.BlockSpec((block, joined), lambda j: (j, 0))] * chips,
        out_specs=[pl.BlockSpec((rows, block), lambda j: (0, j))] * 2,
        out_shape=[jax.ShapeDtypeStruct((rows, features), BF)] * 2,
        compiler_params=params(1),
        name="backward_second",
    )(d_joined, inner, *weights)


def forward_first(parts, weights):
    rows, count = parts[0].shape[0], len(parts)
    features, joined = weights[0].shape
    chips = len(weights)
    hidden = joined // 2
    block = 1792
    steps = features // block

    def body(*refs):
        row_refs, refs = refs[:count], refs[count:]
        out_ref, total = refs[chips:]
        step = pl.program_id(0)
        right = jnp.concatenate([ref[...] for ref in refs[:chips]], axis=1)
        left = jnp.concatenate([ref[...] for ref in row_refs], axis=0)
        got = contract(left, right, 0)

        @pl.when(step == 0)
        def _():
            total[...] = got

        @pl.when(step > 0)
        def _():
            total[...] += got

        @pl.when(step == steps - 1)
        def _():
            for s in range(chips):
                at = 2 * s * hidden
                gate = total[:, at : at + hidden]
                up = total[:, at + hidden : at + 2 * hidden]
                out_ref[:, s * hidden : (s + 1) * hidden] = (jax.nn.silu(gate) * up).astype(BF)

    return pl.pallas_call(
        body,
        grid=(steps,),
        in_specs=[pl.BlockSpec((rows, block), lambda j: (0, j))] * count
        + [pl.BlockSpec((block, joined), lambda j: (j, 0))] * chips,
        out_specs=pl.BlockSpec((count * rows, chips * hidden), lambda j: (0, 0)),
        out_shape=jax.ShapeDtypeStruct((count * rows, chips * hidden), BF),
        scratch_shapes=[pltpu.VMEM((count * rows, chips * joined), F32)],
        compiler_params=params(1),
        name="forward_first",
    )(*parts, *weights)


def forward_second(hidden_f, downs):
    rows = hidden_f.shape[0] // 2
    hidden, features = downs[0].shape
    chips = len(downs)
    block = 1792

    def body(hidden_ref, *refs):
        keep_ref, give_ref = refs[chips:]
        right = jnp.concatenate([ref[...] for ref in refs[:chips]], axis=0)
        got = contract(hidden_ref[...], right, 0)
        keep_ref[...] = got[:rows].astype(BF)
        give_ref[...] = got[rows:].astype(BF)

    return pl.pallas_call(
        body,
        grid=(features // block,),
        in_specs=[pl.BlockSpec(hidden_f.shape, lambda j: (0, 0))]
        + [pl.BlockSpec((hidden, block), lambda j: (0, j))] * chips,
        out_specs=[pl.BlockSpec((rows, block), lambda j: (0, j))] * 2,
        out_shape=[jax.ShapeDtypeStruct((rows, features), BF)] * 2,
        compiler_params=params(1),
        name="forward_second",
    )(hidden_f, *downs)


def merged(keep, swapped):
    total = (keep.astype(F32) + swapped.astype(F32)).astype(BF)
    return [total[place * CAP : (place + 1) * CAP] for place in (0, 2, 1, 3)]


def combine(picks, factors, returned, rows, extra, name):
    tokens = rows.shape[0]
    features = returned[0].shape[1]
    block = 3584
    top, pieces = len(picks), len(returned)
    slots = picks[0].shape[1]

    def body(*refs):
        pick_refs, factor_ref, refs = refs[:top], refs[top], refs[top + 1 :]
        back_refs, rows_ref, refs = refs[:pieces], refs[pieces], refs[pieces + 1 :]
        out_ref = refs[-1]
        back = jnp.concatenate([ref[...].astype(F32) for ref in back_refs], axis=0).astype(BF)
        total = rows_ref[...].astype(F32)
        for k in range(top):
            picked = jnp.dot(pick_refs[k][...], back, preferred_element_type=F32)
            total += factor_ref[:, k : k + 1] * picked
        if extra is not None:
            score_ref, router_ref = refs[:2]
            for e in range(extra[1].shape[0]):
                total += score_ref[:, e : e + 1] * router_ref[e : e + 1, :].astype(F32)
        out_ref[...] = total.astype(BF)

    in_specs = (
        [pl.BlockSpec((tokens, slots), lambda j: (0, 0))] * top
        + [pl.BlockSpec(factors.shape, lambda j: (0, 0))]
        + [pl.BlockSpec((CAP, block), lambda j: (0, j)) for _ in range(pieces)]
        + [pl.BlockSpec((tokens, block), lambda j: (0, j))]
    )
    operands = list(picks) + [factors] + list(returned) + [rows]
    if extra is not None:
        in_specs += [
            pl.BlockSpec(extra[0].shape, lambda j: (0, 0)),
            pl.BlockSpec((extra[1].shape[0], block), lambda j: (0, j)),
        ]
        operands += list(extra)
    return pl.pallas_call(
        body,
        grid=(features // block,),
        in_specs=in_specs,
        out_specs=pl.BlockSpec((tokens, block), lambda j: (0, j)),
        out_shape=jax.ShapeDtypeStruct((tokens, features), BF),
        compiler_params=params(1),
        name=name,
    )(*operands)


def shards(
    forward_rows,
    forward_ids,
    backward_rows,
    backward_ids,
    backward_grad,
    backward_stash,
    router,
    w_gate,
    w_up,
    w_down,
):
    fwd_rows, fwd_ids = forward_rows[0], forward_ids[0]
    bwd_rows, bwd_ids, bwd_grad = backward_rows[0], backward_ids[0], backward_grad[0]
    router_rows = router[0]
    gate_w, up_w, down_w = w_gate[0, 0], w_up[0, 0], w_down[0, 0]
    members = lax.axis_size("expert")
    experts, features = router_rows.shape
    hidden = down_w.shape[0]
    tokens, top = fwd_ids.shape
    slots = experts * CAP
    index = lax.axis_index("expert")
    level = index // 4
    core = jnp.reshape(index % 2, (1,))
    chip = jnp.reshape(level % 2 * 2 + index // 2 % 2, (1,))
    slot_axis = jnp.arange(slots, dtype=jnp.int32)

    joined_w = jnp.concatenate([gate_w, up_w], axis=1)

    slot_f = route_plan(fwd_ids, experts, level)
    slot_b = route_plan(bwd_ids, experts, level)
    select_f = jnp.sum(slot_axis[:, None, None] == slot_f[None], axis=2).astype(BF)
    select_b = jnp.sum(slot_axis[:, None, None] == slot_b[None], axis=2).astype(BF)
    pairs_b = (slot_axis[:, None] == slot_b.reshape(1, tokens * top)).astype(BF)
    stash = backward_stash[0].reshape(tokens * top, 2 * backward_stash.shape[-1])
    sent = pack(core, select_f, select_b, pairs_b, fwd_rows, bwd_grad, stash, hidden)
    near, far = sent

    first = hopped(far, 2)
    down_y, down_z = exchanged(down_w, 2), exchanged(down_w, 4)
    joined_y, joined_z = exchanged(joined_w, 2), exchanged(joined_w, 4)
    first, down_y, joined_z, down_z, joined_y = lax.optimization_barrier(
        (first, down_y, joined_z, down_z, joined_y)
    )

    own_1 = jnp.concatenate([near[:CAP], first[:CAP]], axis=0)
    own_2 = hopped(jnp.concatenate([near[CAP:], first[CAP:]], axis=0), 1)
    other_1 = exchanged(own_1, 1)
    cut = hidden // 3 // 16 * 16
    down_d = [exchanged(down_z[:cut], 2), exchanged(down_y[cut:], 4)]
    joined_d = exchanged(joined_z, 2)
    own_2, other_1, down_d, joined_d = lax.optimization_barrier((own_2, other_1, down_d, joined_d))
    parts = [own_1, own_2, other_1, exchanged(own_2, 1)]
    downs = [down_w, down_y, down_z, jnp.concatenate(down_d, axis=0)]
    joins = [joined_w, joined_y, joined_z, joined_d]

    d_joined, inner = backward_first(chip, parts, downs)
    keep, give = backward_second(d_joined, inner, joins)
    pieces = merged(keep, exchanged(give, 1))
    _, probs_f, total_f = gate_terms(fwd_rows, fwd_ids, router_rows)
    weights_f = ROUTE_SCALE * probs_f / total_f
    plan_f = shifted(jnp.concatenate([slot_f.astype(F32), weights_f], axis=1), "pipe", 1)
    parts, pieces, plan_f = lax.optimization_barrier((parts, pieces, plan_f))
    next_rows = shifted(fwd_rows, "pipe", 1)
    back_b = [to_source(rows, k) for k, rows in enumerate(pieces)]
    hidden_f = forward_first(parts, joins)
    keep, give = forward_second(hidden_f, downs)
    swapped = exchanged(give, 1)
    back_f = [to_next(rows, k) for k, rows in enumerate(merged(keep, swapped))]

    back_b, next_rows = lax.optimization_barrier((back_b, next_rows))
    one_hot_b, probs_b, total_b = gate_terms(bwd_rows, bwd_ids, router_rows)
    share_b = probs_b / total_b
    scale_b = (ROUTE_SCALE * share_b).astype(BF).astype(F32)
    picks_b = [(slot_b[:, k : k + 1] == slot_axis[None, :]).astype(BF) for k in range(top)]
    inner_all = jnp.concatenate([rows[USED : USED + 1, :CAP] for rows in back_b], axis=1)
    inner_all = inner_all.astype(F32)
    inner_sum = jnp.stack(
        [jnp.sum(picks_b[k].astype(F32) * inner_all, axis=1) for k in range(top)], axis=1
    )
    d_logit = (
        ROUTE_SCALE
        / total_b
        * (inner_sum - jnp.sum(share_b * inner_sum, axis=1, keepdims=True))
        * probs_b
        * (1.0 - probs_b)
    )
    score_grad = jnp.sum(one_hot_b * d_logit[:, :, None], axis=1)
    router_total = jnp.dot(score_grad.T, bwd_rows.astype(F32), precision=lax.Precision.HIGHEST)
    router_total = router_total * (1.0 / (tokens * members))
    shares = jnp.transpose(router_total.reshape(experts, members, features // members), (1, 0, 2))
    shares = all_to_all(shares)
    extra = (score_grad, router_rows)
    input_grad = combine(picks_b, scale_b, back_b, bwd_grad, extra, "combine_backward")
    backward_out_rows = shifted(input_grad, "pipe", -1)
    back_f, _ = lax.optimization_barrier((back_f, input_grad))

    slot_f, weights_f = plan_f[:, :top].astype(jnp.int32), plan_f[:, top:]
    picks_f = [(slot_f[:, k : k + 1] == slot_axis[None, :]).astype(BF) for k in range(top)]
    layer_out = combine(picks_f, weights_f, back_f, next_rows, None, "combine_forward")
    shares, layer_out = lax.optimization_barrier((shares, layer_out))
    shares = all_to_all(jnp.broadcast_to(jnp.sum(shares, axis=0)[None], shares.shape))
    router_total = jnp.transpose(shares, (1, 0, 2)).reshape(experts, features)
    return (layer_out[None], backward_out_rows[None], router_total[None])


def solution(mesh):
    return jax.shard_map(
        shards,
        mesh=mesh,
        in_specs=(
            P("pipe", "expert", None),
            P("pipe", "expert", None),
            P("pipe", "expert", None),
            P("pipe", "expert", None),
            P("pipe", "expert", None),
            P("pipe", "expert", None, None, None),
            P("pipe", None, None),
            P("pipe", "expert", None, None),
            P("pipe", "expert", None, None),
            P("pipe", "expert", None, None),
        ),
        out_specs=(P("pipe", "expert", None), P("pipe", "expert", None), P("pipe", None, None)),
        check_vma=False,
    )
```

```python
import jax
import jax.numpy as jnp
from jax import lax
from jax.experimental import pallas as pl
from jax.experimental.pallas import tpu as pltpu
from jax.sharding import PartitionSpec as P

CAP = 40
ROUTE_SCALE = 2.5
BF = jnp.bfloat16
F32 = jnp.float32
USED = 36
VMEM_BYTES = 48 * 1024 * 1024


def params(steps):
    return pltpu.CompilerParams(
        dimension_semantics=("arbitrary",) * steps, vmem_limit_bytes=VMEM_BYTES
    )


def shifted(block, axis, distance):
    devices = range(lax.axis_size(axis))
    route = [((i - distance) % len(devices), i) for i in devices]
    return lax.ppermute(block, axis, route)


def exchanged(block, mask):
    route = [(i, i ^ mask) for i in range(lax.axis_size("expert"))]
    return lax.ppermute(block, "expert", route)


def all_to_all(block):
    return lax.all_to_all(block, "expert", split_axis=0, concat_axis=0, tiled=True)


def piece_route(piece):
    members = lax.axis_size("expert")
    step = (0, 2, -1, -3)[piece]
    return [(i, (i + 4 * (step if i // 4 % 2 == 0 else -step)) % members) for i in range(members)]


def hopped(block, piece):
    return lax.ppermute(block, "expert", piece_route(piece))


def to_source(block, piece):
    if not piece:
        return block
    return lax.ppermute(block, "expert", [(b, a) for a, b in piece_route(piece)])


def gate_terms(tok_rows, ids, router_rows):
    experts = router_rows.shape[0]
    logits = lax.dot_general(
        tok_rows, router_rows, (((1,), (1,)), ((), ())), preferred_element_type=F32
    )
    one_hot = (ids[:, :, None] == jnp.arange(experts, dtype=jnp.int32)[None, None, :]).astype(F32)
    probs_m = jax.nn.sigmoid(jnp.sum(one_hot * logits[:, None, :], axis=2))
    total_m = jnp.sum(probs_m, axis=1, keepdims=True)
    return one_hot, probs_m, total_m


def route_plan(ids, experts, level):
    tokens, top = ids.shape
    flat_ids = ids.reshape(tokens * top)
    one_hot = (flat_ids[:, None] == jnp.arange(experts, dtype=jnp.int32)[None, :]).astype(jnp.int32)
    before = jnp.cumsum(one_hot, axis=0) - one_hot
    rank = jnp.sum(before * one_hot, axis=1)
    ahead = flat_ids - level // 2
    ahead = jnp.where(level % 2 == 0, ahead, -ahead) % experts
    piece = jnp.where(ahead == 2, 3, jnp.where(ahead == 3, 2, ahead))
    return (piece * CAP + rank).reshape(tokens, top)


def pack(core, select_f, select_b, select_pairs, rows_f, rows_b, stash, hidden):
    tokens, features = rows_f.shape
    slots, pairs = select_pairs.shape
    lanes = stash.shape[1]
    quarter = lanes // 4
    chips = quarter // hidden
    total = 2 * features + lanes
    block = total // 4

    def body(core_ref, f_ref, b_ref, pairs_ref, rows_f_ref, rows_b_ref, stash_ref, *out_refs):
        def spread(select_ref, source, at):
            got = jnp.dot(select_ref[...], source, preferred_element_type=F32)
            for k in range(2):
                half = got[k * slots // 2 : (k + 1) * slots // 2]
                out_refs[k][:, at : at + source.shape[1]] = half.astype(BF)

        def fill(step):
            first, last = step * block, (step + 1) * block
            for select_ref, ref, start in ((f_ref, rows_f_ref, 0), (b_ref, rows_b_ref, features)):
                low, high = max(first, start), min(last, start + features)
                if low < high:
                    spread(select_ref, ref[:, low - start : high - start], low - first)
            for place in range(4 * chips):
                at = 2 * features + place * hidden
                if first <= at < last:
                    owner = (core_ref[0] + 1 + place // (2 * chips)) % 2
                    part, chip = place // chips % 2, place % chips
                    start = part * 2 * quarter + (2 * chip + owner) * hidden
                    source = stash_ref[:, pl.ds(pl.multiple_of(start, hidden), hidden)]
                    spread(pairs_ref, source, at - first)

        for step in range(4):
            pl.when(pl.program_id(0) == step)(lambda step=step: fill(step))

    def whole(array):
        return pl.BlockSpec(array.shape, lambda j: (0, 0))

    return pl.pallas_call(
        body,
        grid=(4,),
        in_specs=[pl.BlockSpec(memory_space=pltpu.SMEM)]
        + [whole(a) for a in (select_f, select_b, select_pairs, rows_f, rows_b, stash)],
        out_specs=[pl.BlockSpec((slots // 2, block), lambda j: (0, j))] * 2,
        out_shape=[jax.ShapeDtypeStruct((slots // 2, total), BF)] * 2,
        compiler_params=params(1),
        name="pack",
    )(core, select_f, select_b, select_pairs, rows_f, rows_b, stash)


def contract(left, right, right_dim):
    return lax.dot_general(left, right, (((1,), (right_dim,)), ((), ())), preferred_element_type=F32)


def silu_slope(pre_act):
    sigmoid_v = jax.nn.sigmoid(pre_act)
    return sigmoid_v * (1.0 + pre_act * (1.0 - sigmoid_v))


def backward_first(chip, parts, downs):
    rows = parts[0].shape[0]
    chips, count = len(downs), len(parts)
    hidden, features = downs[0].shape
    block = 1792
    steps = features // block
    wide = 2 * chips * hidden

    def body(chip_ref, *refs):
        row_refs, stash_refs, refs = refs[:count], refs[count : 2 * count], refs[2 * count :]
        w_refs, (d_ref, inner_ref, total) = refs[:chips], refs[chips:]
        step = pl.program_id(0)
        left = jnp.concatenate([ref[...] for ref in row_refs], axis=0)
        right = jnp.concatenate([ref[...] for ref in w_refs], axis=0)
        got = contract(left, right, 1)

        @pl.when(step == 0)
        def _():
            total[...] = got

        @pl.when(step > 0)
        def _():
            total[...] += got

        @pl.when(step == steps - 1)
        def _():
            for part, stash_ref in enumerate(stash_refs):
                place = slice(part * rows, (part + 1) * rows)
                products = jnp.zeros((rows, hidden), F32)
                for s in range(chips):
                    start = (chip_ref[0] ^ s) * hidden
                    pre_gate = stash_ref[:, pl.ds(pl.multiple_of(start, hidden), hidden)].astype(F32)
                    start = start + chips * hidden
                    pre_up = stash_ref[:, pl.ds(pl.multiple_of(start, hidden), hidden)].astype(F32)
                    raw = total[place, s * hidden : (s + 1) * hidden]
                    sigmoid_v = jax.nn.sigmoid(pre_gate)
                    activated = pre_gate * sigmoid_v
                    slope = sigmoid_v * (1.0 + pre_gate * (1.0 - sigmoid_v))
                    hidden_b = (activated * pre_up).astype(BF).astype(F32)
                    products += hidden_b * raw
                    at = 2 * s * hidden
                    d_ref[place, at : at + hidden] = (raw * pre_up * slope).astype(BF)
                    d_ref[place, at + hidden : at + 2 * hidden] = (raw * activated).astype(BF)
                high = products.astype(BF)
                low = (products - high.astype(F32)).astype(BF)
                ones = jnp.ones((8, hidden), BF)
                for k in range(rows // CAP):
                    piece = slice(k * CAP, (k + 1) * CAP)
                    inner = contract(ones, high[piece], 1) + contract(ones, low[piece], 1)
                    inner = jnp.pad(inner, ((0, 0), (0, hidden - CAP)))
                    at = 8 * (part * rows // CAP + k)
                    inner_ref[at : at + 8, :] = inner

    return pl.pallas_call(
        body,
        grid=(steps,),
        in_specs=[pl.BlockSpec(memory_space=pltpu.SMEM)]
        + [pl.BlockSpec((rows, block), lambda j: (0, steps + j))] * count
        + [pl.BlockSpec((rows, wide), lambda j: (0, 2 * features // wide + 1))] * (count // 2)
        + [pl.BlockSpec((rows, wide), lambda j: (0, 2 * features // wide))] * (count // 2)
        + [pl.BlockSpec((hidden, block), lambda j: (0, j))] * chips,
        out_specs=[
            pl.BlockSpec((count * rows, 2 * chips * hidden), lambda j: (0, 0)),
            pl.BlockSpec((count * rows // CAP * 8, hidden), lambda j: (0, 0)),
        ],
        out_shape=[
            jax.ShapeDtypeStruct((count * rows, 2 * chips * hidden), BF),
            jax.ShapeDtypeStruct((count * rows // CAP * 8, hidden), F32),
        ],
        scratch_shapes=[pltpu.VMEM((count * rows, chips * hidden), F32)],
        compiler_params=params(1),
        name="backward_first",
    )(chip, *parts, *parts, *downs)


def backward_second(d_joined, inner, weights):
    rows = d_joined.shape[0] // 2
    features, joined = weights[0].shape
    chips = len(weights)
    block = 1792
    lanes = inner.shape[1]

    def body(d_ref, inner_ref, *refs):
        out_refs = refs[chips:]
        right = jnp.concatenate([ref[...] for ref in refs[:chips]], axis=1)
        got = contract(d_ref[...], right, 1)
        for half, out_ref in enumerate(out_refs):
            out_ref[...] = got[half * rows : (half + 1) * rows].astype(BF)

        @pl.when(pl.program_id(0) == 0)
        def _():
            used = lax.broadcasted_iota(jnp.int32, (CAP, lanes), 0) == USED
            for half, out_ref in enumerate(out_refs):
                pieces = []
                for k in range(half * rows // CAP, (half + 1) * rows // CAP):
                    piece = got[k * CAP : (k + 1) * CAP, :lanes]
                    pieces.append(jnp.where(used, inner_ref[8 * k : 8 * k + 1, :], piece))
                out_ref[:, :lanes] = jnp.concatenate(pieces, axis=0).astype(BF)

    return pl.pallas_call(
        body,
        grid=(features // block,),
        in_specs=[pl.BlockSpec(a.shape, lambda j: (0, 0)) for a in (d_joined, inner)]
        + [pl.BlockSpec((block, joined), lambda j: (j, 0))] * chips,
        out_specs=[pl.BlockSpec((rows, block), lambda j: (0, j))] * 2,
        out_shape=[jax.ShapeDtypeStruct((rows, features), BF)] * 2,
        compiler_params=params(1),
        name="backward_second",
    )(d_joined, inner, *weights)


def forward_first(parts, weights):
    rows, count = parts[0].shape[0], len(parts)
    features, joined = weights[0].shape
    chips = len(weights)
    hidden = joined // 2
    block = 1792
    steps = features // block

    def body(*refs):
        row_refs, refs = refs[:count], refs[count:]
        out_ref, total = refs[chips:]
        step = pl.program_id(0)
        right = jnp.concatenate([ref[...] for ref in refs[:chips]], axis=1)
        left = jnp.concatenate([ref[...] for ref in row_refs], axis=0)
        got = contract(left, right, 0)

        @pl.when(step == 0)
        def _():
            total[...] = got

        @pl.when(step > 0)
        def _():
            total[...] += got

        @pl.when(step == steps - 1)
        def _():
            for s in range(chips):
                at = 2 * s * hidden
                gate = total[:, at : at + hidden]
                up = total[:, at + hidden : at + 2 * hidden]
                out_ref[:, s * hidden : (s + 1) * hidden] = (jax.nn.silu(gate) * up).astype(BF)

    return pl.pallas_call(
        body,
        grid=(steps,),
        in_specs=[pl.BlockSpec((rows, block), lambda j: (0, j))] * count
        + [pl.BlockSpec((block, joined), lambda j: (j, 0))] * chips,
        out_specs=pl.BlockSpec((count * rows, chips * hidden), lambda j: (0, 0)),
        out_shape=jax.ShapeDtypeStruct((count * rows, chips * hidden), BF),
        scratch_shapes=[pltpu.VMEM((count * rows, chips * joined), F32)],
        compiler_params=params(1),
        name="forward_first",
    )(*parts, *weights)


def forward_second(hidden_f, downs):
    rows = hidden_f.shape[0] // 2
    hidden, features = downs[0].shape
    chips = len(downs)
    block = 1792

    def body(hidden_ref, *refs):
        keep_ref, give_ref = refs[chips:]
        right = jnp.concatenate([ref[...] for ref in refs[:chips]], axis=0)
        got = contract(hidden_ref[...], right, 0)
        keep_ref[...] = got[:rows].astype(BF)
        give_ref[...] = got[rows:].astype(BF)

    return pl.pallas_call(
        body,
        grid=(features // block,),
        in_specs=[pl.BlockSpec(hidden_f.shape, lambda j: (0, 0))]
        + [pl.BlockSpec((hidden, block), lambda j: (0, j))] * chips,
        out_specs=[pl.BlockSpec((rows, block), lambda j: (0, j))] * 2,
        out_shape=[jax.ShapeDtypeStruct((rows, features), BF)] * 2,
        compiler_params=params(1),
        name="forward_second",
    )(hidden_f, *downs)


def merged(keep, swapped):
    places = [slice(place * CAP, (place + 1) * CAP) for place in (0, 2, 1, 3)]
    return [(keep[at].astype(F32) + swapped[at].astype(F32)).astype(BF) for at in places]


def combine(picks, factors, returned, rows, extra, name):
    tokens = rows.shape[0]
    features = returned[0].shape[1]
    block = 3584
    top, pieces = len(picks), len(returned)
    slots = picks[0].shape[1]

    def body(*refs):
        pick_refs, factor_ref, refs = refs[:top], refs[top], refs[top + 1 :]
        back_refs, rows_ref, refs = refs[:pieces], refs[pieces], refs[pieces + 1 :]
        out_ref = refs[-1]
        back = jnp.concatenate([ref[...].astype(F32) for ref in back_refs], axis=0).astype(BF)
        total = rows_ref[...].astype(F32)
        for k in range(top):
            picked = jnp.dot(pick_refs[k][...], back, preferred_element_type=F32)
            total += factor_ref[:, k : k + 1] * picked
        if extra is not None:
            score_ref, router_ref = refs[:2]
            for e in range(extra[1].shape[0]):
                total += score_ref[:, e : e + 1] * router_ref[e : e + 1, :].astype(F32)
        out_ref[...] = total.astype(BF)

    in_specs = (
        [pl.BlockSpec((tokens, slots), lambda j: (0, 0))] * top
        + [pl.BlockSpec(factors.shape, lambda j: (0, 0))]
        + [pl.BlockSpec((CAP, block), lambda j: (0, j)) for _ in range(pieces)]
        + [pl.BlockSpec((tokens, block), lambda j: (0, j))]
    )
    operands = list(picks) + [factors] + list(returned) + [rows]
    if extra is not None:
        in_specs += [
            pl.BlockSpec(extra[0].shape, lambda j: (0, 0)),
            pl.BlockSpec((extra[1].shape[0], block), lambda j: (0, j)),
        ]
        operands += list(extra)
    return pl.pallas_call(
        body,
        grid=(features // block,),
        in_specs=in_specs,
        out_specs=pl.BlockSpec((tokens, block), lambda j: (0, j)),
        out_shape=jax.ShapeDtypeStruct((tokens, features), BF),
        compiler_params=params(1),
        name=name,
    )(*operands)


def shards(
    forward_rows,
    forward_ids,
    backward_rows,
    backward_ids,
    backward_grad,
    backward_stash,
    router,
    w_gate,
    w_up,
    w_down,
):
    fwd_rows, fwd_ids = forward_rows[0], forward_ids[0]
    bwd_rows, bwd_ids, bwd_grad = backward_rows[0], backward_ids[0], backward_grad[0]
    router_rows = router[0]
    gate_w, up_w, down_w = w_gate[0, 0], w_up[0, 0], w_down[0, 0]
    members = lax.axis_size("expert")
    experts, features = router_rows.shape
    hidden = down_w.shape[0]
    tokens, top = fwd_ids.shape
    slots = experts * CAP
    index = lax.axis_index("expert")
    level = index // 4
    core = jnp.reshape(index % 2, (1,))
    chip = jnp.reshape(level % 2 * 2 + index // 2 % 2, (1,))
    slot_axis = jnp.arange(slots, dtype=jnp.int32)

    joined_w = jnp.concatenate([gate_w, up_w], axis=1)

    slot_f = route_plan(fwd_ids, experts, level)
    slot_b = route_plan(bwd_ids, experts, level)
    select_f = jnp.sum(slot_axis[:, None, None] == slot_f[None], axis=2).astype(BF)
    select_b = jnp.sum(slot_axis[:, None, None] == slot_b[None], axis=2).astype(BF)
    pairs_b = (slot_axis[:, None] == slot_b.reshape(1, tokens * top)).astype(BF)
    stash = backward_stash[0].reshape(tokens * top, 2 * backward_stash.shape[-1])
    sent = pack(core, select_f, select_b, pairs_b, fwd_rows, bwd_grad, stash, hidden)
    near, far = sent

    first = hopped(far, 2)
    down_y, down_z = exchanged(down_w, 2), exchanged(down_w, 4)
    joined_y, joined_z = exchanged(joined_w, 2), exchanged(joined_w, 4)
    first, down_y, joined_z, down_z, joined_y = lax.optimization_barrier(
        (first, down_y, joined_z, down_z, joined_y)
    )

    own_1 = jnp.concatenate([near[:CAP], first[:CAP]], axis=0)
    own_2 = hopped(jnp.concatenate([near[CAP:], first[CAP:]], axis=0), 1)
    other_1 = exchanged(own_1, 1)
    cut = hidden // 3 // 16 * 16
    down_d = [exchanged(down_z[:cut], 2), exchanged(down_y[cut:], 4)]
    joined_d = exchanged(joined_z, 2)
    own_2, other_1, down_d, joined_d = lax.optimization_barrier((own_2, other_1, down_d, joined_d))
    parts = [own_1, own_2, other_1, exchanged(own_2, 1)]
    downs = [down_w, down_y, down_z, jnp.concatenate(down_d, axis=0)]
    joins = [joined_w, joined_y, joined_z, joined_d]

    d_joined, inner = backward_first(chip, parts, downs)
    keep, give = backward_second(d_joined, inner, joins)
    pieces = merged(keep, exchanged(give, 1))
    parts, pieces = lax.optimization_barrier((parts, pieces))
    back_b = [to_source(rows, k) for k, rows in enumerate(pieces)]
    hidden_f = forward_first(parts, joins)
    keep, give = forward_second(hidden_f, downs)
    swapped = exchanged(give, 1)
    back_f = [to_source(rows, k) for k, rows in enumerate(merged(keep, swapped))]

    back_b = lax.optimization_barrier(back_b)
    one_hot_b, probs_b, total_b = gate_terms(bwd_rows, bwd_ids, router_rows)
    share_b = probs_b / total_b
    scale_b = (ROUTE_SCALE * share_b).astype(BF).astype(F32)
    picks_b = [(slot_b[:, k : k + 1] == slot_axis[None, :]).astype(BF) for k in range(top)]
    inner_all = jnp.concatenate([rows[USED : USED + 1, :CAP] for rows in back_b], axis=1)
    inner_all = inner_all.astype(F32)
    inner_sum = jnp.stack(
        [jnp.sum(picks_b[k].astype(F32) * inner_all, axis=1) for k in range(top)], axis=1
    )
    d_logit = (
        ROUTE_SCALE
        / total_b
        * (inner_sum - jnp.sum(share_b * inner_sum, axis=1, keepdims=True))
        * probs_b
        * (1.0 - probs_b)
    )
    score_grad = jnp.sum(one_hot_b * d_logit[:, :, None], axis=1)
    router_total = jnp.dot(score_grad.T, bwd_rows.astype(F32), precision=lax.Precision.HIGHEST)
    router_total = router_total * (1.0 / (tokens * members))
    shares = jnp.transpose(router_total.reshape(experts, members, features // members), (1, 0, 2))
    shares = all_to_all(shares)
    extra = (score_grad, router_rows)
    input_grad = combine(picks_b, scale_b, back_b, bwd_grad, extra, "combine_backward")
    backward_out_rows = shifted(input_grad, "pipe", -1)
    back_f, _ = lax.optimization_barrier((back_f, input_grad))

    one_hot_f, probs_f, total_f = gate_terms(fwd_rows, fwd_ids, router_rows)
    weights_f = ROUTE_SCALE * probs_f / total_f
    picks_f = [(slot_f[:, k : k + 1] == slot_axis[None, :]).astype(BF) for k in range(top)]
    layer_out = combine(picks_f, weights_f, back_f, fwd_rows, None, "combine_forward")
    shares, layer_out = lax.optimization_barrier((shares, layer_out))
    shares = all_to_all(jnp.broadcast_to(jnp.sum(shares, axis=0)[None], shares.shape))
    router_total = jnp.transpose(shares, (1, 0, 2)).reshape(experts, features)
    forward_out_rows = shifted(layer_out, "pipe", 1)
    return (forward_out_rows[None], backward_out_rows[None], router_total[None])


def solution(mesh):
    return jax.shard_map(
        shards,
        mesh=mesh,
        in_specs=(
            P("pipe", "expert", None),
            P("pipe", "expert", None),
            P("pipe", "expert", None),
            P("pipe", "expert", None),
            P("pipe", "expert", None),
            P("pipe", "expert", None, None, None),
            P("pipe", None, None),
            P("pipe", "expert", None, None),
            P("pipe", "expert", None, None),
            P("pipe", "expert", None, None),
        ),
        out_specs=(P("pipe", "expert", None), P("pipe", "expert", None), P("pipe", None, None)),
        check_vma=False,
    )
```

```python
import jax
import jax.numpy as jnp
from jax import lax
from jax.experimental import pallas as pl
from jax.experimental.pallas import tpu as pltpu
from jax.sharding import PartitionSpec as P

CAP = 40
ROUTE_SCALE = 2.5
BF = jnp.bfloat16
F32 = jnp.float32
USED = 36
VMEM_BYTES = 48 * 1024 * 1024


def params(steps):
    return pltpu.CompilerParams(
        dimension_semantics=("arbitrary",) * steps, vmem_limit_bytes=VMEM_BYTES
    )


def shifted(block, axis, distance):
    devices = range(lax.axis_size(axis))
    route = [((i - distance) % len(devices), i) for i in devices]
    return lax.ppermute(block, axis, route)


def exchanged(block, mask):
    route = [(i, i ^ mask) for i in range(lax.axis_size("expert"))]
    return lax.ppermute(block, "expert", route)


def all_to_all(block):
    return lax.all_to_all(block, "expert", split_axis=0, concat_axis=0, tiled=True)


def piece_route(piece):
    members = lax.axis_size("expert")
    step = (0, 2, -1, -3)[piece]
    return [(i, (i + 4 * (step if i // 4 % 2 == 0 else -step)) % members) for i in range(members)]


def hopped(block, piece):
    return lax.ppermute(block, "expert", piece_route(piece))


def to_source(block, piece):
    if not piece:
        return block
    return lax.ppermute(block, "expert", [(b, a) for a, b in piece_route(piece)])


def gate_terms(tok_rows, ids, router_rows):
    experts = router_rows.shape[0]
    logits = lax.dot_general(
        tok_rows, router_rows, (((1,), (1,)), ((), ())), preferred_element_type=F32
    )
    one_hot = (ids[:, :, None] == jnp.arange(experts, dtype=jnp.int32)[None, None, :]).astype(F32)
    probs_m = jax.nn.sigmoid(jnp.sum(one_hot * logits[:, None, :], axis=2))
    total_m = jnp.sum(probs_m, axis=1, keepdims=True)
    return one_hot, probs_m, total_m


def route_plan(ids, experts, level):
    tokens, top = ids.shape
    flat_ids = ids.reshape(tokens * top)
    one_hot = (flat_ids[:, None] == jnp.arange(experts, dtype=jnp.int32)[None, :]).astype(jnp.int32)
    before = jnp.cumsum(one_hot, axis=0) - one_hot
    rank = jnp.sum(before * one_hot, axis=1)
    ahead = flat_ids - level // 2
    ahead = jnp.where(level % 2 == 0, ahead, -ahead) % experts
    piece = jnp.where(ahead == 2, 3, jnp.where(ahead == 3, 2, ahead))
    return (piece * CAP + rank).reshape(tokens, top)


def pack(core, select_f, select_b, select_pairs, rows_f, rows_b, stash, hidden):
    tokens, features = rows_f.shape
    slots, pairs = select_pairs.shape
    lanes = stash.shape[1]
    quarter = lanes // 4
    chips = quarter // hidden
    total = 2 * features + lanes
    block = total // 4

    def body(core_ref, f_ref, b_ref, pairs_ref, rows_f_ref, rows_b_ref, stash_ref, *out_refs):
        def spread(select_ref, source, at):
            got = jnp.dot(select_ref[...], source, preferred_element_type=F32)
            for k in range(2):
                half = got[k * slots // 2 : (k + 1) * slots // 2]
                out_refs[k][:, at : at + source.shape[1]] = half.astype(BF)

        def fill(step):
            first, last = step * block, (step + 1) * block
            for select_ref, ref, start in ((f_ref, rows_f_ref, 0), (b_ref, rows_b_ref, features)):
                low, high = max(first, start), min(last, start + features)
                if low < high:
                    spread(select_ref, ref[:, low - start : high - start], low - first)
            for place in range(4 * chips):
                at = 2 * features + place * hidden
                if first <= at < last:
                    owner = (core_ref[0] + 1 + place // (2 * chips)) % 2
                    part, chip = place // chips % 2, place % chips
                    start = part * 2 * quarter + (2 * chip + owner) * hidden
                    source = stash_ref[:, pl.ds(pl.multiple_of(start, hidden), hidden)]
                    spread(pairs_ref, source, at - first)

        for step in range(4):
            pl.when(pl.program_id(0) == step)(lambda step=step: fill(step))

    def whole(array):
        return pl.BlockSpec(array.shape, lambda j: (0, 0))

    return pl.pallas_call(
        body,
        grid=(4,),
        in_specs=[pl.BlockSpec(memory_space=pltpu.SMEM)]
        + [whole(a) for a in (select_f, select_b, select_pairs, rows_f, rows_b, stash)],
        out_specs=[pl.BlockSpec((slots // 2, block), lambda j: (0, j))] * 2,
        out_shape=[jax.ShapeDtypeStruct((slots // 2, total), BF)] * 2,
        compiler_params=params(1),
        name="pack",
    )(core, select_f, select_b, select_pairs, rows_f, rows_b, stash)


def contract(left, right, right_dim):
    return lax.dot_general(left, right, (((1,), (right_dim,)), ((), ())), preferred_element_type=F32)


def silu_slope(pre_act):
    sigmoid_v = jax.nn.sigmoid(pre_act)
    return sigmoid_v * (1.0 + pre_act * (1.0 - sigmoid_v))


def backward_first(chip, parts, downs):
    rows = parts[0].shape[0]
    chips, count = len(downs), len(parts)
    hidden, features = downs[0].shape
    block = 1792
    steps = features // block
    wide = 2 * chips * hidden

    def body(chip_ref, *refs):
        row_refs, stash_refs, refs = refs[:count], refs[count : 2 * count], refs[2 * count :]
        w_refs, (d_ref, inner_ref, total) = refs[:chips], refs[chips:]
        step = pl.program_id(0)
        left = jnp.concatenate([ref[...] for ref in row_refs], axis=0)
        right = jnp.concatenate([ref[...] for ref in w_refs], axis=0)
        got = contract(left, right, 1)

        @pl.when(step == 0)
        def _():
            total[...] = got

        @pl.when(step > 0)
        def _():
            total[...] += got

        @pl.when(step == steps - 1)
        def _():
            for part, stash_ref in enumerate(stash_refs):
                place = slice(part * rows, (part + 1) * rows)
                products = jnp.zeros((rows, hidden), F32)
                for s in range(chips):
                    start = (chip_ref[0] ^ s) * hidden
                    pre_gate = stash_ref[:, pl.ds(pl.multiple_of(start, hidden), hidden)].astype(F32)
                    start = start + chips * hidden
                    pre_up = stash_ref[:, pl.ds(pl.multiple_of(start, hidden), hidden)].astype(F32)
                    raw = total[place, s * hidden : (s + 1) * hidden]
                    sigmoid_v = jax.nn.sigmoid(pre_gate)
                    activated = pre_gate * sigmoid_v
                    slope = sigmoid_v * (1.0 + pre_gate * (1.0 - sigmoid_v))
                    hidden_b = (activated * pre_up).astype(BF).astype(F32)
                    products += hidden_b * raw
                    at = 2 * s * hidden
                    d_ref[place, at : at + hidden] = (raw * pre_up * slope).astype(BF)
                    d_ref[place, at + hidden : at + 2 * hidden] = (raw * activated).astype(BF)
                high = products.astype(BF)
                low = (products - high.astype(F32)).astype(BF)
                ones = jnp.ones((8, hidden), BF)
                for k in range(rows // CAP):
                    piece = slice(k * CAP, (k + 1) * CAP)
                    inner = contract(ones, high[piece], 1) + contract(ones, low[piece], 1)
                    inner = jnp.pad(inner, ((0, 0), (0, hidden - CAP)))
                    at = 8 * (part * rows // CAP + k)
                    inner_ref[at : at + 8, :] = inner

    return pl.pallas_call(
        body,
        grid=(steps,),
        in_specs=[pl.BlockSpec(memory_space=pltpu.SMEM)]
        + [pl.BlockSpec((rows, block), lambda j: (0, steps + j))] * count
        + [pl.BlockSpec((rows, wide), lambda j: (0, 2 * features // wide + 1))] * (count // 2)
        + [pl.BlockSpec((rows, wide), lambda j: (0, 2 * features // wide))] * (count // 2)
        + [pl.BlockSpec((hidden, block), lambda j: (0, j))] * chips,
        out_specs=[
            pl.BlockSpec((count * rows, 2 * chips * hidden), lambda j: (0, 0)),
            pl.BlockSpec((count * rows // CAP * 8, hidden), lambda j: (0, 0)),
        ],
        out_shape=[
            jax.ShapeDtypeStruct((count * rows, 2 * chips * hidden), BF),
            jax.ShapeDtypeStruct((count * rows // CAP * 8, hidden), F32),
        ],
        scratch_shapes=[pltpu.VMEM((count * rows, chips * hidden), F32)],
        compiler_params=params(1),
        name="backward_first",
    )(chip, *parts, *parts, *downs)


def backward_second(d_joined, inner, weights):
    rows = d_joined.shape[0] // 2
    features, joined = weights[0].shape
    chips = len(weights)
    block = 1792
    lanes = inner.shape[1]

    def body(d_ref, inner_ref, *refs):
        out_refs = refs[chips:]
        right = jnp.concatenate([ref[...] for ref in refs[:chips]], axis=1)
        got = contract(d_ref[...], right, 1)
        for half, out_ref in enumerate(out_refs):
            out_ref[...] = got[half * rows : (half + 1) * rows].astype(BF)

        @pl.when(pl.program_id(0) == 0)
        def _():
            used = lax.broadcasted_iota(jnp.int32, (CAP, lanes), 0) == USED
            for half, out_ref in enumerate(out_refs):
                pieces = []
                for k in range(half * rows // CAP, (half + 1) * rows // CAP):
                    piece = got[k * CAP : (k + 1) * CAP, :lanes]
                    pieces.append(jnp.where(used, inner_ref[8 * k : 8 * k + 1, :], piece))
                out_ref[:, :lanes] = jnp.concatenate(pieces, axis=0).astype(BF)

    return pl.pallas_call(
        body,
        grid=(features // block,),
        in_specs=[pl.BlockSpec(a.shape, lambda j: (0, 0)) for a in (d_joined, inner)]
        + [pl.BlockSpec((block, joined), lambda j: (j, 0))] * chips,
        out_specs=[pl.BlockSpec((rows, block), lambda j: (0, j))] * 2,
        out_shape=[jax.ShapeDtypeStruct((rows, features), BF)] * 2,
        compiler_params=params(1),
        name="backward_second",
    )(d_joined, inner, *weights)


def forward_first(parts, weights):
    rows, count = parts[0].shape[0], len(parts)
    features, joined = weights[0].shape
    chips = len(weights)
    hidden = joined // 2
    block = 1792
    steps = features // block

    def body(*refs):
        row_refs, refs = refs[:count], refs[count:]
        out_ref, total = refs[chips:]
        step = pl.program_id(0)
        right = jnp.concatenate([ref[...] for ref in refs[:chips]], axis=1)
        left = jnp.concatenate([ref[...] for ref in row_refs], axis=0)
        got = contract(left, right, 0)

        @pl.when(step == 0)
        def _():
            total[...] = got

        @pl.when(step > 0)
        def _():
            total[...] += got

        @pl.when(step == steps - 1)
        def _():
            for s in range(chips):
                at = 2 * s * hidden
                gate = total[:, at : at + hidden]
                up = total[:, at + hidden : at + 2 * hidden]
                out_ref[:, s * hidden : (s + 1) * hidden] = (jax.nn.silu(gate) * up).astype(BF)

    return pl.pallas_call(
        body,
        grid=(steps,),
        in_specs=[pl.BlockSpec((rows, block), lambda j: (0, j))] * count
        + [pl.BlockSpec((block, joined), lambda j: (j, 0))] * chips,
        out_specs=pl.BlockSpec((count * rows, chips * hidden), lambda j: (0, 0)),
        out_shape=jax.ShapeDtypeStruct((count * rows, chips * hidden), BF),
        scratch_shapes=[pltpu.VMEM((count * rows, chips * joined), F32)],
        compiler_params=params(1),
        name="forward_first",
    )(*parts, *weights)


def forward_second(hidden_f, downs):
    rows = hidden_f.shape[0] // 2
    hidden, features = downs[0].shape
    chips = len(downs)
    block = 1792

    def body(hidden_ref, *refs):
        keep_ref, give_ref = refs[chips:]
        right = jnp.concatenate([ref[...] for ref in refs[:chips]], axis=0)
        got = contract(hidden_ref[...], right, 0)
        keep_ref[...] = got[:rows].astype(BF)
        give_ref[...] = got[rows:].astype(BF)

    return pl.pallas_call(
        body,
        grid=(features // block,),
        in_specs=[pl.BlockSpec(hidden_f.shape, lambda j: (0, 0))]
        + [pl.BlockSpec((hidden, block), lambda j: (0, j))] * chips,
        out_specs=[pl.BlockSpec((rows, block), lambda j: (0, j))] * 2,
        out_shape=[jax.ShapeDtypeStruct((rows, features), BF)] * 2,
        compiler_params=params(1),
        name="forward_second",
    )(hidden_f, *downs)


def merged(keep, swapped):
    places = [slice(place * CAP, (place + 1) * CAP) for place in (0, 2, 1, 3)]
    return [(keep[at].astype(F32) + swapped[at].astype(F32)).astype(BF) for at in places]


def combine(picks, factors, returned, rows, extra, name):
    tokens = rows.shape[0]
    features = returned[0].shape[1]
    block = 3584
    top, pieces = len(picks), len(returned)
    slots = picks[0].shape[1]

    def body(*refs):
        pick_refs, factor_ref, refs = refs[:top], refs[top], refs[top + 1 :]
        back_refs, rows_ref, refs = refs[:pieces], refs[pieces], refs[pieces + 1 :]
        out_ref = refs[-1]
        back = jnp.concatenate([ref[...].astype(F32) for ref in back_refs], axis=0).astype(BF)
        total = rows_ref[...].astype(F32)
        for k in range(top):
            picked = jnp.dot(pick_refs[k][...], back, preferred_element_type=F32)
            total += factor_ref[:, k : k + 1] * picked
        if extra is not None:
            score_ref, router_ref = refs[:2]
            for e in range(extra[1].shape[0]):
                total += score_ref[:, e : e + 1] * router_ref[e : e + 1, :].astype(F32)
        out_ref[...] = total.astype(BF)

    in_specs = (
        [pl.BlockSpec((tokens, slots), lambda j: (0, 0))] * top
        + [pl.BlockSpec(factors.shape, lambda j: (0, 0))]
        + [pl.BlockSpec((CAP, block), lambda j: (0, j)) for _ in range(pieces)]
        + [pl.BlockSpec((tokens, block), lambda j: (0, j))]
    )
    operands = list(picks) + [factors] + list(returned) + [rows]
    if extra is not None:
        in_specs += [
            pl.BlockSpec(extra[0].shape, lambda j: (0, 0)),
            pl.BlockSpec((extra[1].shape[0], block), lambda j: (0, j)),
        ]
        operands += list(extra)
    return pl.pallas_call(
        body,
        grid=(features // block,),
        in_specs=in_specs,
        out_specs=pl.BlockSpec((tokens, block), lambda j: (0, j)),
        out_shape=jax.ShapeDtypeStruct((tokens, features), BF),
        compiler_params=params(1),
        name=name,
    )(*operands)


def shards(
    forward_rows,
    forward_ids,
    backward_rows,
    backward_ids,
    backward_grad,
    backward_stash,
    router,
    w_gate,
    w_up,
    w_down,
):
    fwd_rows, fwd_ids = forward_rows[0], forward_ids[0]
    bwd_rows, bwd_ids, bwd_grad = backward_rows[0], backward_ids[0], backward_grad[0]
    router_rows = router[0]
    gate_w, up_w, down_w = w_gate[0, 0], w_up[0, 0], w_down[0, 0]
    members = lax.axis_size("expert")
    experts, features = router_rows.shape
    hidden = down_w.shape[0]
    tokens, top = fwd_ids.shape
    slots = experts * CAP
    index = lax.axis_index("expert")
    level = index // 4
    core = jnp.reshape(index % 2, (1,))
    chip = jnp.reshape(level % 2 * 2 + index // 2 % 2, (1,))
    slot_axis = jnp.arange(slots, dtype=jnp.int32)

    joined_w = jnp.concatenate([gate_w, up_w], axis=1)

    slot_f = route_plan(fwd_ids, experts, level)
    slot_b = route_plan(bwd_ids, experts, level)
    select_f = jnp.sum(slot_axis[:, None, None] == slot_f[None], axis=2).astype(BF)
    select_b = jnp.sum(slot_axis[:, None, None] == slot_b[None], axis=2).astype(BF)
    pairs_b = (slot_axis[:, None] == slot_b.reshape(1, tokens * top)).astype(BF)
    stash = backward_stash[0].reshape(tokens * top, 2 * backward_stash.shape[-1])
    sent = pack(core, select_f, select_b, pairs_b, fwd_rows, bwd_grad, stash, hidden)
    near, far = sent

    first = hopped(far, 2)
    down_y, down_z = exchanged(down_w, 2), exchanged(down_w, 4)
    joined_y, joined_z = exchanged(joined_w, 2), exchanged(joined_w, 4)
    first, down_y, joined_z, down_z, joined_y = lax.optimization_barrier(
        (first, down_y, joined_z, down_z, joined_y)
    )

    own_1 = jnp.concatenate([near[:CAP], first[:CAP]], axis=0)
    own_2 = hopped(jnp.concatenate([near[CAP:], first[CAP:]], axis=0), 1)
    other_1 = exchanged(own_1, 1)
    cut = hidden // 8
    down_d = [exchanged(down_z[:cut], 2), exchanged(down_y[cut:], 4)]
    joined_d = exchanged(joined_z, 2)
    own_2, other_1, down_d, joined_d = lax.optimization_barrier((own_2, other_1, down_d, joined_d))
    parts = [own_1, own_2, other_1, exchanged(own_2, 1)]
    downs = [down_w, down_y, down_z, jnp.concatenate(down_d, axis=0)]
    joins = [joined_w, joined_y, joined_z, joined_d]

    d_joined, inner = backward_first(chip, parts, downs)
    keep, give = backward_second(d_joined, inner, joins)
    pieces = merged(keep, exchanged(give, 1))
    parts, pieces = lax.optimization_barrier((parts, pieces))
    back_b = [to_source(rows, k) for k, rows in enumerate(pieces)]
    hidden_f = forward_first(parts, joins)
    keep, give = forward_second(hidden_f, downs)
    swapped = exchanged(give, 1)
    back_f = [to_source(rows, k) for k, rows in enumerate(merged(keep, swapped))]

    back_b = lax.optimization_barrier(back_b)
    one_hot_b, probs_b, total_b = gate_terms(bwd_rows, bwd_ids, router_rows)
    share_b = probs_b / total_b
    scale_b = (ROUTE_SCALE * share_b).astype(BF).astype(F32)
    picks_b = [(slot_b[:, k : k + 1] == slot_axis[None, :]).astype(BF) for k in range(top)]
    inner_all = jnp.concatenate([rows[USED : USED + 1, :CAP] for rows in back_b], axis=1)
    inner_all = inner_all.astype(F32)
    inner_sum = jnp.stack(
        [jnp.sum(picks_b[k].astype(F32) * inner_all, axis=1) for k in range(top)], axis=1
    )
    d_logit = (
        ROUTE_SCALE
        / total_b
        * (inner_sum - jnp.sum(share_b * inner_sum, axis=1, keepdims=True))
        * probs_b
        * (1.0 - probs_b)
    )
    score_grad = jnp.sum(one_hot_b * d_logit[:, :, None], axis=1)
    router_total = jnp.dot(score_grad.T, bwd_rows.astype(F32), precision=lax.Precision.HIGHEST)
    router_total = router_total * (1.0 / (tokens * members))
    shares = jnp.transpose(router_total.reshape(experts, members, features // members), (1, 0, 2))
    shares = all_to_all(shares)
    extra = (score_grad, router_rows)
    input_grad = combine(picks_b, scale_b, back_b, bwd_grad, extra, "combine_backward")
    backward_out_rows = shifted(input_grad, "pipe", -1)
    back_f, _ = lax.optimization_barrier((back_f, input_grad))

    one_hot_f, probs_f, total_f = gate_terms(fwd_rows, fwd_ids, router_rows)
    weights_f = ROUTE_SCALE * probs_f / total_f
    picks_f = [(slot_f[:, k : k + 1] == slot_axis[None, :]).astype(BF) for k in range(top)]
    layer_out = combine(picks_f, weights_f, back_f, fwd_rows, None, "combine_forward")
    shares, layer_out = lax.optimization_barrier((shares, layer_out))
    shares = all_to_all(jnp.broadcast_to(jnp.sum(shares, axis=0)[None], shares.shape))
    router_total = jnp.transpose(shares, (1, 0, 2)).reshape(experts, features)
    forward_out_rows = shifted(layer_out, "pipe", 1)
    return (forward_out_rows[None], backward_out_rows[None], router_total[None])


def solution(mesh):
    return jax.shard_map(
        shards,
        mesh=mesh,
        in_specs=(
            P("pipe", "expert", None),
            P("pipe", "expert", None),
            P("pipe", "expert", None),
            P("pipe", "expert", None),
            P("pipe", "expert", None),
            P("pipe", "expert", None, None, None),
            P("pipe", None, None),
            P("pipe", "expert", None, None),
            P("pipe", "expert", None, None),
            P("pipe", "expert", None, None),
        ),
        out_specs=(P("pipe", "expert", None), P("pipe", "expert", None), P("pipe", None, None)),
        check_vma=False,
    )
```
